256 devices in a mesh: phase: 2 (over z_lo), slab: 4 (over y), tile: 32 (over z_hi, x, core).
Axes of the slice: x: 4, y: 4, z: 8 (z_hi: 4, z_lo: 2; z = z_hi * 2 + z_lo), core: 2. Of those that a mesh axis runs over, the one named last changes fastest.
Arguments:
- volume: float32 [128, 1024, 512], P('slab', 'tile'), may hold values from -6 to 6
- frac: float32 [2, 1024, 512], P('phase', 'tile'), may hold values from 0 to 1
- shift: int32 [2, 1024], P('phase', 'tile'), may hold values from -16 to 15
- angle_index: int32 [2, 32], P('phase'), may hold values from 0 to 679
- depth_weights: float32 [680, 128], P(None, 'slab'), may hold values from -0.5 to 0.5
- measured: float32 [2, 32, 1024, 512], P('phase', None, 'tile'), may hold values from -6 to 6
Outputs:
- image_grad: float32 [128, 1024, 512], P('slab', 'tile')
- field_grad: float32 [2, 1024, 512], P('phase', 'tile')
The draws below stay inside these ranges and needn't reach their ends.
All inputs are finite; a program needn't handle non-finite values.
Results may differ from the reference program's by a relative error of at most 0.0001.
Values sent between devices are 32-bit elements; how exact they have to be, the bound alone decides.
No kernel may reach another device: no remote copies, remote signals or barrier semaphores. Data moves between devices by JAX's collectives and lax.ppermute only.
A program may use at most 128 MiB of HBM per device.

```python
import jax
import jax.numpy as jnp
from jax import lax

H = 512
ANG = 32
NANG = 680
HALO = 16
ITS = 4
D = 128
L = 1024
NPH = 2


def set_ends(result, own_key, low, high):
    index_at = [jax.random.randint(jax.random.fold_in(own_key, axis), (), 0, length) for axis, length in enumerate(result.shape)]
    main_axis = result.shape.index(max(result.shape))
    beside = index_at[:main_axis] + [(index_at[main_axis] + 1) % result.shape[main_axis]] + index_at[main_axis + 1:]
    return result.at[tuple(index_at)].set(low).at[tuple(beside)].set(high)


def level_of(stream_key, shape, split, least, high):
    def one(dim, parts):
        draws = jax.random.uniform(jax.random.fold_in(jax.random.fold_in(stream_key, 6), dim), (parts,), jnp.float32, least / len(split), high / len(split))
        return jnp.repeat(jnp.exp(draws), shape[dim] // parts).reshape((-1,) + (1,) * (len(shape) - dim - 1))

    gain = one(*split[0])
    for cut in split[1:]:
        gain = gain * one(*cut)
    return gain


def scatter_about(stream_key, extent, deviation, limit, shards=(), held_as=jnp.bfloat16):
    factor_of = level_of(stream_key, extent, shards, -0.22, 0.18) if shards else 1.0
    entries = jax.random.normal(stream_key, extent, jnp.float32) * deviation * factor_of
    return jnp.minimum(jnp.maximum(entries, -limit), limit).astype(held_as)


def setup_inputs(seed: int = 0) -> dict:
    seeds = jax.random.split(jax.random.key(seed), 7)
    volume = scatter_about(seeds[0], (D, L, H), 1.0, 6.0, ((0, 4), (1, 32)), jnp.float32)
    frac = jnp.clip(1.0 * jax.random.uniform(seeds[1], (NPH, L, H), jnp.float32) ** level_of(seeds[1], (NPH, L, H), ((0, 2), (1, 32)), -0.2, 0.2), 0.0, 1.0)
    shift = set_ends(jax.random.randint(seeds[2], (NPH, L), -HALO, HALO), jax.random.fold_in(seeds[2], 1), -HALO, HALO - 1).astype(jnp.int32)
    angle_index = set_ends(jax.random.randint(seeds[3], (NPH, ANG), 0, NANG), jax.random.fold_in(seeds[3], 1), 0, NANG - 1).astype(jnp.int32)
    depth_weights = scatter_about(seeds[4], (NANG, D), D ** -0.5, 0.5, ((1, 4),), jnp.float32)
    measured = scatter_about(seeds[5], (NPH, ANG, L, H), 1.0, 6.0, ((0, 2), (2, 32)), jnp.float32)
    return {"volume": volume, "frac": frac, "shift": shift, "angle_index": angle_index, "depth_weights": depth_weights, "measured": measured}


DIFFUSION = 0.2

def warp_image(image, frac_phase, shift_phase):
    padded = jnp.pad(image, ((0, 0), (HALO, HALO), (0, 0)))
    columns = jnp.arange(L, dtype=jnp.int32) + HALO + shift_phase.astype(jnp.int32)
    lower = jnp.take(padded, columns, axis=1)
    upper = jnp.take(padded, columns + 1, axis=1)
    return (1.0 - frac_phase)[None] * lower + frac_phase[None] * upper

def diffuse(field):
    for sweep in range(ITS):
        padded = jnp.pad(field, ((0, 0), (1, 1), (1, 1)))
        laplace = padded[:, 2:, 1:-1] + padded[:, :-2, 1:-1] + padded[:, 1:-1, 2:] + padded[:, 1:-1, :-2] - 4.0 * field
        field = field + DIFFUSION * laplace
    return field

def reference(volume, frac, shift, angle_index, depth_weights, measured):
    image_grad = jnp.zeros(volume.shape, jnp.float32)
    fields = []
    for member in range(NPH):
        weights = jnp.take(depth_weights, angle_index[member], axis=0)
        shift_phase = shift[member]
        warped, pullback = jax.vjp(lambda image, part: warp_image(image, part, shift_phase), volume, frac[member])
        flat_warp = warped.reshape(D, L * H)
        projected = jnp.dot(weights, flat_warp, precision=lax.Precision.HIGHEST)
        residual = projected - measured[member].reshape(ANG, L * H)
        spread = jnp.dot(weights.T, residual, precision=lax.Precision.HIGHEST).reshape(D, L, H)
        grad_image, grad_frac = pullback(spread)
        image_grad = image_grad + grad_image
        fields.append(grad_frac)
    field_grad = diffuse(jnp.stack(fields))
    return (image_grad, field_grad)
```

```python
import jax
import jax.numpy as jnp
from jax import lax
from jax.experimental import pallas as pl
from jax.experimental.pallas import tpu as pltpu
from jax.sharding import PartitionSpec as P

HALO = 16
ITS = 4
DIFFUSION = 0.2
EDGE = 8
LANES = 128
HIGH = lax.Precision.HIGHEST
F32 = jnp.float32
VMEM = pl.BlockSpec(memory_space=pltpu.VMEM)
SMEM = pl.BlockSpec(memory_space=pltpu.SMEM)


def call(kernel, outs, in_specs, scratch=(), limit=16, flops=1 << 22, moved=1 << 22):
    return pl.pallas_call(
        kernel,
        out_shape=[jax.ShapeDtypeStruct(o, F32) for o in outs],
        in_specs=in_specs,
        out_specs=[VMEM] * len(outs),
        scratch_shapes=list(scratch),
        compiler_params=pltpu.CompilerParams(vmem_limit_bytes=limit << 20),
        cost_estimate=pl.CostEstimate(flops=flops, bytes_accessed=moved, transcendentals=0),
    )


def outer(a, b, precision=HIGH):
    return lax.dot_general(
        a, b, (((0,), (0,)), ((), ())), precision=precision, preferred_element_type=F32
    )


def project(place, index, table, volume, out):
    depth, cols, _ = volume.shape
    rows = table.shape[1]
    picker = (
        lax.broadcasted_iota(jnp.int32, (rows, index.shape[1]), 0) == index[...]
    ).astype(F32)
    flipped = jnp.dot(table[...], picker, precision=HIGH, preferred_element_type=F32)
    row = lax.broadcasted_iota(jnp.int32, (depth, LANES), 0)
    lane = lax.broadcasted_iota(jnp.int32, (depth, LANES), 1)
    shifted = outer(flipped, (lane == row + place[0] * depth).astype(F32))
    weights = outer(flipped, (lane == row).astype(F32))[:, :depth]
    for chunk in range(out.shape[0]):
        out[chunk, cols] = shifted
    for base in range(0, cols, 8):
        block = jnp.swapaxes(volume[:, base : base + 8, :], 0, 1)
        for k in range(8):
            part = jnp.dot(weights, block[k], precision=HIGH, preferred_element_type=F32)
            for chunk in range(out.shape[0]):
                out[chunk, base + k] = part[:, chunk * LANES : (chunk + 1) * LANES]


def gather_parts(parts, low, high, weights):
    cols = parts.shape[1] - 1
    half = cols // 2

    def total(k):
        return (parts[0, k] + parts[1, k]) + (parts[2, k] + parts[3, k])

    for k in range(half):
        low[k] = total(k)
        high[k] = total(half + k)
    weights[...] = total(cols)


def turn(place, measured, out):
    out[...] = jnp.swapaxes(measured[0], 0, 1)


def residual(shift, left, low, high, right, measured, frac, down, center, up, field, ext, grad):
    cols, angles, width = measured.shape
    ext[0:HALO] = left[...]
    ext[HALO : 2 * HALO] = low[...]
    ext[2 * HALO : 3 * HALO] = high[...]
    ext[3 * HALO :] = right[...]
    grad[...] = jnp.zeros_like(grad)
    for k in range(cols):
        at = k + HALO + shift[0, k]
        lower, upper = ext[at], ext[at + 1]
        part = frac[k : k + 1, :]
        rest = 1.0 - part
        resid = (rest * lower + part * upper) - measured[k]
        field[k : k + 1, :] = jnp.sum(resid * (upper - lower), axis=0, keepdims=True)
        grad[at] = grad[at] + rest * resid
        grad[at + 1] = grad[at + 1] + part * resid
    center[...] = grad[HALO : HALO + cols]
    down[0:HALO] = grad[0:HALO]
    up[0:HALO] = grad[HALO + cols :]
    down[HALO] = jnp.zeros((angles, width), F32)
    up[HALO] = jnp.zeros((angles, width), F32)
    down[HALO, 0:EDGE, :] = field[0:EDGE, :]
    up[HALO, 0:EDGE, :] = field[cols - EDGE : cols, :]


def land(center, left, right, weights, field, out, wide):
    cols = center.shape[0]
    out[0:HALO] = center[0:HALO] + left[0:HALO]
    out[HALO:cols] = center[HALO:cols] + right[0:HALO]
    out[cols] = weights[...]
    wide[0:EDGE] = left[HALO, 0:EDGE, :]
    wide[EDGE : EDGE + cols] = field[...]
    wide[EDGE + cols : cols + 2 * EDGE] = right[HALO, 0:EDGE, :]
    wide[cols + 2 * EDGE :] = jnp.zeros((wide.shape[0] - cols - 2 * EDGE, wide.shape[1]), F32)


def spread(place, own, other, wide, out):
    cols = own.shape[0] - 1
    depth = out.shape[2]
    first = place[1] == 0

    def both(k):
        a, b = own[k], other[k]
        return jnp.concatenate([jnp.where(first, a, b), jnp.where(first, b, a)], axis=0)

    weights = both(cols)
    for k in range(0, cols, 2):
        pair = jnp.concatenate([both(k), both(k + 1)], axis=1)
        value = outer(weights, pair)
        for chunk in range(out.shape[0]):
            rows = value[chunk * depth : (chunk + 1) * depth]
            out[chunk, k] = rows[:, :LANES]
            out[chunk, k + 1] = rows[:, LANES:]
    for chunk in range(out.shape[0]):
        out[chunk, cols] = wide[0:depth]
        out[chunk, cols + 1] = wide[depth:]


def finish(place, last, parts, image, field):
    chunks, rows, depth, width = parts.shape
    cols = rows - 2
    for chunk in range(chunks):
        for base in range(0, cols, 8):
            block = jnp.swapaxes(parts[chunk, base : base + 8], 0, 1)
            image[:, base : base + 8, chunk * width : (chunk + 1) * width] = block
    wide = jnp.concatenate(
        [jnp.concatenate([parts[c, cols], parts[c, cols + 1]], axis=0) for c in range(chunks)],
        axis=1,
    )[: cols + 2 * EDGE]
    height, total = wide.shape
    row = lax.broadcasted_iota(jnp.int32, wide.shape, 0)
    lane = lax.broadcasted_iota(jnp.int32, wide.shape, 1)
    outside = ((row < EDGE) & (place[2] == 0)) | ((row >= EDGE + cols) & (place[2] == last))
    for _ in range(ITS):
        after = pltpu.roll(wide, height - 1, 0)
        before = pltpu.roll(wide, 1, 0)
        right = jnp.where(lane == total - 1, 0.0, pltpu.roll(wide, total - 1, 1))
        left = jnp.where(lane == 0, 0.0, pltpu.roll(wide, 1, 1))
        laplace = after + before + right + left - 4.0 * wide
        wide = jnp.where(outside, 0.0, wide + DIFFUSION * laplace)
    field[0] = wide[EDGE : EDGE + cols]


def shifted(block, distance):
    count = lax.axis_size("tile")
    route = [(i, i + distance) for i in range(count) if 0 <= i + distance < count]
    return lax.ppermute(block, "tile", route)


def body(volume, frac, shift, angle_index, depth_weights, measured):
    depth, cols, height = volume.shape
    angles = angle_index.shape[1]
    slabs = lax.axis_size("slab")
    slab = lax.axis_index("slab")
    place = jnp.stack([slab, lax.axis_index("phase"), lax.axis_index("tile")]).astype(jnp.int32)
    half = (HALO, angles, LANES)
    edge = (HALO + 1, angles, LANES)
    (parts,) = call(
        project, [(slabs, cols + 1, angles, LANES)], [SMEM, VMEM, VMEM, VMEM]
    )(place, angle_index, depth_weights.T, volume)
    parts = lax.all_to_all(parts, "slab", 0, 0, tiled=True)
    low, high, weights = call(gather_parts, [half, half, (angles, LANES)], [VMEM])(parts)
    from_left = shifted(high, 1)
    from_right = shifted(low, -1)
    mine = pl.pallas_call(
        turn,
        out_shape=jax.ShapeDtypeStruct((cols, angles, LANES), F32),
        grid_spec=pltpu.PrefetchScalarGridSpec(
            num_scalar_prefetch=1,
            grid=(1,),
            in_specs=[pl.BlockSpec((1, angles, cols, LANES), lambda i, place: (0, 0, 0, place[0]))],
            out_specs=pl.BlockSpec((cols, angles, LANES), lambda i, place: (0, 0, 0)),
        ),
        cost_estimate=pl.CostEstimate(flops=1 << 20, bytes_accessed=1 << 20, transcendentals=0),
    )(place, measured)
    part = lax.dynamic_slice_in_dim(frac[0], slab * LANES, LANES, axis=1)
    scratch = [pltpu.VMEM((cols + 2 * HALO, angles, LANES), F32)] * 2
    down, center, up, field = call(
        residual,
        [edge, (cols, angles, LANES), edge, (cols, LANES)],
        [SMEM] + [VMEM] * 6,
        scratch,
    )(shift, from_left, low, high, from_right, mine, part)
    left = shifted(up, 1)
    right = shifted(down, -1)
    own, wide = call(
        land, [(cols + 1, angles, LANES), (2 * depth, LANES)], [VMEM] * 5
    )(center, left, right, weights, field)
    phases = lax.axis_size("phase")
    other = lax.ppermute(own, "phase", [(i, phases - 1 - i) for i in range(phases)])
    (parts,) = call(
        spread, [(slabs, cols + 2, depth, LANES)], [SMEM] + [VMEM] * 3
    )(place, own, other, wide)
    parts = lax.all_to_all(parts, "slab", 0, 0, tiled=True)

    def ending(place, parts, image, field):
        finish(place, lax.axis_size("tile") - 1, parts, image, field)

    return call(ending, [(depth, cols, height), (1, cols, height)], [SMEM, VMEM])(place, parts)


def solution(mesh):
    return jax.shard_map(
        body,
        mesh=mesh,
        in_specs=(
            P("slab", "tile", None),
            P("phase", "tile", None),
            P("phase", "tile"),
            P("phase", None),
            P(None, "slab"),
            P("phase", None, "tile", None),
        ),
        out_specs=(P("slab", "tile", None), P("phase", "tile", None)),
        check_vma=False,
    )
```

```python
import jax
import jax.numpy as jnp
from jax import lax
from jax.experimental import pallas as pl
from jax.experimental.pallas import tpu as pltpu
from jax.sharding import PartitionSpec as P

HALO = 16
ITS = 4
DIFFUSION = 0.2
EDGE = 8
ALONE = 8
LANES = 128
HIGH = lax.Precision.HIGHEST
F32 = jnp.float32
VMEM = pl.BlockSpec(memory_space=pltpu.VMEM)
SMEM = pl.BlockSpec(memory_space=pltpu.SMEM)


def call(kernel, outs, in_specs, scratch=(), limit=16, flops=1 << 22, moved=1 << 22):
    return pl.pallas_call(
        kernel,
        out_shape=[jax.ShapeDtypeStruct(o, F32) for o in outs],
        in_specs=in_specs,
        out_specs=[VMEM] * len(outs),
        scratch_shapes=list(scratch),
        compiler_params=pltpu.CompilerParams(vmem_limit_bytes=limit << 20),
        cost_estimate=pl.CostEstimate(flops=flops, bytes_accessed=moved, transcendentals=0),
    )


def outer(a, b, precision=HIGH):
    return lax.dot_general(
        a, b, (((0,), (0,)), ((), ())), precision=precision, preferred_element_type=F32
    )


def cut(place, volume, out):
    out[0, 0 : volume.shape[1]] = jnp.swapaxes(volume[...], 0, 1)


def pick(place, index, other, table, partial, out):
    depth, rows = table.shape
    angles = index.shape[1]
    number = lax.broadcasted_iota(jnp.int32, (rows, angles), 0)
    row = lax.broadcasted_iota(jnp.int32, (depth, LANES), 0)
    lane = lax.broadcasted_iota(jnp.int32, (depth, LANES), 1)
    target = (lane == row + place[0] * depth).astype(F32)
    for k, name in enumerate((index, other)):
        picker = (number == name[...]).astype(F32)
        flipped = jnp.dot(table[...], picker, precision=HIGH, preferred_element_type=F32)
        weights = outer(flipped, target)
        for chunk in range(out.shape[0]):
            out[chunk, HALO + k] = weights


def project(parts, own, other, weights):
    slabs = parts.shape[0]
    angles = own.shape[1]

    def over(k):
        return jnp.concatenate([parts[s, k] for s in range(slabs)], axis=0)

    def total(k):
        return (parts[0, k] + parts[1, k]) + (parts[2, k] + parts[3, k])

    table = jnp.concatenate([total(HALO), total(HALO + 1)], axis=0)
    weights[...] = table
    for k in range(0, HALO, 2):
        pair = jnp.concatenate([over(k), over(k + 1)], axis=1)
        value = jnp.dot(table, pair, precision=HIGH, preferred_element_type=F32)
        own[k] = value[:angles, :LANES]
        own[k + 1] = value[:angles, LANES:]
        other[k] = value[angles:, :LANES]
        other[k + 1] = value[angles:, LANES:]


def turn(place, measured, out):
    out[...] = jnp.swapaxes(measured[0], 0, 1)


def residual(place, shift, own, partner, same, crossed, measured, frac, down, center, up, field, ext, grad):
    cols, angles, width = measured.shape
    phase = place[1]
    ext[pl.ds(HALO * (1 + phase), HALO)] = own[...]
    ext[pl.ds(HALO * (2 - phase), HALO)] = partner[...]
    ext[pl.ds(3 * HALO * (1 - phase), HALO)] = same[...]
    ext[pl.ds(3 * HALO * phase, HALO)] = crossed[...]
    grad[...] = jnp.zeros_like(grad)
    for k in range(cols):
        at = k + HALO + shift[0, k]
        lower, upper = ext[at], ext[at + 1]
        part = frac[k : k + 1, :]
        rest = 1.0 - part
        resid = (rest * lower + part * upper) - measured[k]
        field[k : k + 1, :] = jnp.sum(resid * (upper - lower), axis=0, keepdims=True)
        grad[at] = grad[at] + rest * resid
        grad[at + 1] = grad[at + 1] + part * resid
    center[...] = grad[HALO : HALO + cols]
    down[0:HALO] = grad[0:HALO]
    up[0:HALO] = grad[HALO + cols :]
    down[HALO] = jnp.zeros((angles, width), F32)
    up[HALO] = jnp.zeros((angles, width), F32)
    down[HALO, 0:EDGE, :] = field[0:EDGE, :]
    up[HALO, 0:EDGE, :] = field[cols - EDGE : cols, :]


def land(place, center, left, right, field, out, alone, shared, wide):
    cols = center.shape[0]
    out[0:HALO] = center[0:HALO] + left[0:HALO]
    out[HALO:cols] = center[HALO:cols] + right[0:HALO]
    alone[...] = out[pl.ds((cols - ALONE) * (1 - place[1]), ALONE)]
    shared[...] = out[ALONE : cols - ALONE]
    wide[0:EDGE] = left[HALO, 0:EDGE, :]
    wide[EDGE : EDGE + cols] = field[...]
    wide[EDGE + cols : cols + 2 * EDGE] = right[HALO, 0:EDGE, :]
    wide[cols + 2 * EDGE :] = jnp.zeros((wide.shape[0] - cols - 2 * EDGE, wide.shape[1]), F32)


def spread(weights, both, cols, out):
    depth = out.shape[2]
    for k in range(0, cols, 2):
        pair = jnp.concatenate([both(k), both(k + 1)], axis=1)
        value = outer(weights, pair)
        for chunk in range(out.shape[0]):
            rows = value[chunk * depth : (chunk + 1) * depth]
            out[chunk, k] = rows[:, :LANES]
            out[chunk, k + 1] = rows[:, LANES:]


def spread_alone(place, weights, own, other, out):
    base = (own.shape[0] - ALONE) * place[1]

    def both(k):
        return jnp.concatenate([own[base + k], other[k]], axis=0)

    spread(weights[...], both, ALONE, out)


def spread_shared(place, weights, own, other, wide, out):
    cols = other.shape[0]
    angles = own.shape[1]
    depth = out.shape[2]
    first = place[1] == 0

    def order(a, b):
        return jnp.concatenate([jnp.where(first, a, b), jnp.where(first, b, a)], axis=0)

    def both(k):
        return order(own[ALONE + k], other[k])

    spread(order(weights[0:angles], weights[angles:]), both, cols, out)
    for chunk in range(out.shape[0]):
        out[chunk, cols] = wide[0:depth]
        out[chunk, cols + 1] = wide[depth:]


def finish(place, last, mine, theirs, parts, image, field):
    chunks, rows, depth, width = parts.shape
    middle = rows - 2
    cols = image.shape[1]
    near = pl.multiple_of((cols - ALONE) * place[1], 8)
    far = pl.multiple_of((cols - ALONE) * (1 - place[1]), 8)
    for chunk in range(chunks):
        lanes = slice(chunk * width, (chunk + 1) * width)
        image[:, pl.ds(near, ALONE), lanes] = jnp.swapaxes(mine[chunk], 0, 1)
        image[:, pl.ds(far, ALONE), lanes] = jnp.swapaxes(theirs[chunk], 0, 1)
        for base in range(0, middle, 8):
            block = jnp.swapaxes(parts[chunk, base : base + 8], 0, 1)
            image[:, ALONE + base : ALONE + base + 8, lanes] = block
    wide = jnp.concatenate(
        [
            jnp.concatenate([parts[c, middle], parts[c, middle + 1]], axis=0)
            for c in range(chunks)
        ],
        axis=1,
    )[: cols + 2 * EDGE]
    height, total = wide.shape
    row = lax.broadcasted_iota(jnp.int32, wide.shape, 0)
    lane = lax.broadcasted_iota(jnp.int32, wide.shape, 1)
    outside = ((row < EDGE) & (place[2] == 0)) | ((row >= EDGE + cols) & (place[2] == last))
    for _ in range(ITS):
        after = pltpu.roll(wide, height - 1, 0)
        before = pltpu.roll(wide, 1, 0)
        right = jnp.where(lane == total - 1, 0.0, pltpu.roll(wide, total - 1, 1))
        left = jnp.where(lane == 0, 0.0, pltpu.roll(wide, 1, 1))
        laplace = after + before + right + left - 4.0 * wide
        wide = jnp.where(outside, 0.0, wide + DIFFUSION * laplace)
    field[0] = wide[EDGE : EDGE + cols]


def move(block, target):
    phases, tiles = lax.axis_size("phase"), lax.axis_size("tile")
    route = []
    for phase in range(phases):
        for tile in range(tiles):
            to_phase, to_tile = target(phase, tile)
            if 0 <= to_tile < tiles:
                route.append((phase * tiles + tile, to_phase * tiles + to_tile))
    return lax.ppermute(block, ("phase", "tile"), route)


def body(volume, frac, shift, angle_index, depth_weights, measured):
    depth, cols, height = volume.shape
    angles = angle_index.shape[1]
    slabs = lax.axis_size("slab")
    slab = lax.axis_index("slab")
    place = jnp.stack([slab, lax.axis_index("phase"), lax.axis_index("tile")]).astype(jnp.int32)
    half = (HALO, angles, LANES)
    edge = (HALO + 1, angles, LANES)
    message = (slabs, HALO + 2, depth, LANES)

    def partner(block):
        return move(block, lambda phase, tile: (1 - phase, tile))

    def away(phase, tile):
        return tile + 2 * phase - 1

    other_index = partner(angle_index)
    cuts = pl.pallas_call(
        cut,
        out_shape=jax.ShapeDtypeStruct(message, F32),
        grid_spec=pltpu.PrefetchScalarGridSpec(
            num_scalar_prefetch=1,
            grid=(slabs,),
            in_specs=[pl.BlockSpec((depth, HALO, LANES), lambda i, place: (0, place[1], i))],
            out_specs=pl.BlockSpec((1,) + message[1:], lambda i, place: (i, 0, 0, 0)),
        ),
        cost_estimate=pl.CostEstimate(flops=1 << 20, bytes_accessed=1 << 22, transcendentals=0),
    )(place, volume)
    message_out = pl.pallas_call(
        pick,
        out_shape=jax.ShapeDtypeStruct(message, F32),
        in_specs=[SMEM, VMEM, VMEM, VMEM, VMEM],
        out_specs=VMEM,
        input_output_aliases={4: 0},
        compiler_params=pltpu.CompilerParams(vmem_limit_bytes=16 << 20),
    )(place, angle_index, other_index, depth_weights.T, cuts)
    parts = lax.all_to_all(message_out, "slab", 0, 0, tiled=True)
    own, other, weights = call(project, [half, half, (2 * angles, LANES)], [VMEM])(parts)
    crossed = move(other, lambda phase, tile: (1 - phase, away(phase, tile)))
    same = move(own, lambda phase, tile: (phase, away(phase, tile)))
    across = partner(other)
    mine = pl.pallas_call(
        turn,
        out_shape=jax.ShapeDtypeStruct((cols, angles, LANES), F32),
        grid_spec=pltpu.PrefetchScalarGridSpec(
            num_scalar_prefetch=1,
            grid=(1,),
            in_specs=[pl.BlockSpec((1, angles, cols, LANES), lambda i, place: (0, 0, 0, place[0]))],
            out_specs=pl.BlockSpec((cols, angles, LANES), lambda i, place: (0, 0, 0)),
        ),
        cost_estimate=pl.CostEstimate(flops=1 << 20, bytes_accessed=1 << 20, transcendentals=0),
    )(place, measured)
    part = lax.dynamic_slice_in_dim(frac[0], slab * LANES, LANES, axis=1)
    scratch = [pltpu.VMEM((cols + 2 * HALO, angles, LANES), F32)] * 2
    down, center, up, field = call(
        residual,
        [edge, (cols, angles, LANES), edge, (cols, LANES)],
        [SMEM] * 2 + [VMEM] * 6,
        scratch,
    )(place, shift, own, across, same, crossed, mine, part)
    left = move(up, lambda phase, tile: (phase, tile + 1))
    right = move(down, lambda phase, tile: (phase, tile - 1))
    alone = (ALONE, angles, LANES)
    shared = (cols - 2 * ALONE, angles, LANES)
    adjoint, alone_out, shared_out, wide = call(
        land,
        [(cols, angles, LANES), alone, shared, (2 * depth, LANES)],
        [SMEM] + [VMEM] * 4,
    )(place, center, left, right, field)
    alone_in = partner(alone_out)
    shared_in = partner(shared_out)
    (first,) = call(spread_alone, [(slabs, ALONE, depth, LANES)], [SMEM] + [VMEM] * 3)(
        place, weights, adjoint, alone_in
    )
    near = lax.all_to_all(first, "slab", 0, 0, tiled=True)
    far = partner(near)
    (second,) = call(
        spread_shared, [(slabs, shared[0] + 2, depth, LANES)], [SMEM] + [VMEM] * 4
    )(place, weights, adjoint, shared_in, wide)
    middle = lax.all_to_all(second, "slab", 0, 0, tiled=True)

    def ending(place, near, far, middle, image, field):
        finish(place, lax.axis_size("tile") - 1, near, far, middle, image, field)

    return call(ending, [(depth, cols, height), (1, cols, height)], [SMEM] + [VMEM] * 3)(
        place, near, far, middle
    )


def solution(mesh):
    return jax.shard_map(
        body,
        mesh=mesh,
        in_specs=(
            P("slab", "tile", None),
            P("phase", "tile", None),
            P("phase", "tile"),
            P("phase", None),
            P(None, "slab"),
            P("phase", None, "tile", None),
        ),
        out_specs=(P("slab", "tile", None), P("phase", "tile", None)),
        check_vma=False,
    )
```

```python
import jax
import jax.numpy as jnp
from jax import lax
from jax.experimental import pallas as pl
from jax.experimental.pallas import tpu as pltpu
from jax.sharding import PartitionSpec as P

HALO = 16
ITS = 4
DIFFUSION = 0.2
EDGE = 8
LANES = 128
ROOM = 56
HIGH = lax.Precision.HIGHEST
F32 = jnp.float32
VMEM = pl.BlockSpec(memory_space=pltpu.VMEM)
SMEM = pl.BlockSpec(memory_space=pltpu.SMEM)
ANY = pl.BlockSpec(memory_space=pltpu.HBM)


def call(kernel, outs, in_specs, scratch=(), out_specs=None, aliases=None, limit=16):
    return pl.pallas_call(
        kernel,
        out_shape=[jax.ShapeDtypeStruct(o, F32) for o in outs],
        in_specs=in_specs,
        out_specs=out_specs or [VMEM] * len(outs),
        scratch_shapes=list(scratch),
        input_output_aliases=aliases or {},
        compiler_params=pltpu.CompilerParams(vmem_limit_bytes=limit << 20),
        cost_estimate=pl.CostEstimate(flops=1 << 22, bytes_accessed=1 << 21, transcendentals=0),
    )


def outer(a, b):
    return lax.dot_general(
        a, b, (((0,), (0,)), ((), ())), precision=HIGH, preferred_element_type=F32
    )


def fetch(volume, base, block, sems):
    copies = []
    for k in range(HALO // 8):
        columns = pl.ds(pl.multiple_of(base + 8 * k, 8), 8)
        copies.append(pltpu.make_async_copy(volume.at[:, columns, :], block.at[k], sems.at[k]))
        copies[k].start()
    return copies


def apply(weights, copies, block, out):
    for k, copy in enumerate(copies):
        copy.wait()
        turned = jnp.swapaxes(block[k], 0, 1)
        for i in range(8):
            part = jnp.dot(weights, turned[i], precision=HIGH, preferred_element_type=F32)
            for chunk in range(out.shape[0]):
                out[chunk, 8 * k + i] = part[:, chunk * LANES : (chunk + 1) * LANES]


def project_first(place, index, table, volume, out, weights, block, sems):
    depth, rows = table.shape
    copies = fetch(volume, HALO * place[3], block, sems)
    picker = (
        lax.broadcasted_iota(jnp.int32, (rows, index.shape[1]), 0) == index[...]
    ).astype(F32)
    flipped = jnp.dot(table[...], picker, precision=HIGH, preferred_element_type=F32)
    row = lax.broadcasted_iota(jnp.int32, (depth, LANES), 0)
    lane = lax.broadcasted_iota(jnp.int32, (depth, LANES), 1)
    moved = outer(flipped, (lane == row + place[0] * depth).astype(F32))
    local = outer(flipped, (lane == row).astype(F32))
    weights[...] = local
    for chunk in range(out.shape[0]):
        out[chunk, HALO] = moved
    apply(local[:, :depth], copies, block, out)


def project_second(place, weights, volume, out, block, sems):
    copies = fetch(volume, HALO * (1 - place[3]), block, sems)
    apply(weights[:, : volume.shape[0]], copies, block, out)


def add_parts(parts, *outs):
    base = 0
    for out in outs:
        for k in range(out.shape[0]):
            low = parts[0, base + k] + parts[1, base + k]
            out[k] = low + (parts[2, base + k] + parts[3, base + k])
        base += out.shape[0]


def turn(place, measured, frac, out, part, block, sems):
    lanes = pl.ds(pl.multiple_of(place[0] * LANES, LANES), LANES)
    first = pltpu.make_async_copy(measured.at[0, :, :, lanes], block, sems.at[0])
    second = pltpu.make_async_copy(frac.at[0, :, lanes], part, sems.at[1])
    first.start()
    second.start()
    first.wait()
    out[...] = jnp.swapaxes(block[...], 0, 1)
    second.wait()


def residual(
    place, shift, own_o, own_e, halo_o, halo_e, measured, frac,
    out_o, out_e, center_o, center_e, field, ext, grad,
):
    odd = place[3]
    cols, angles, width = measured.shape
    at_o, at_e = HALO * (1 + odd), HALO * (2 - odd)
    edge_o, edge_e = 3 * HALO * odd, 3 * HALO * (1 - odd)
    ext[pl.ds(at_o, HALO)] = own_o[...]
    ext[pl.ds(at_e, HALO)] = own_e[...]
    ext[pl.ds(edge_o, HALO)] = halo_o[...]
    ext[pl.ds(edge_e, HALO)] = halo_e[...]
    grad[...] = jnp.zeros_like(grad)
    for k in range(cols):
        at = k + HALO + shift[0, k]
        lower, upper = ext[at], ext[at + 1]
        part = frac[k : k + 1, :]
        rest = 1.0 - part
        resid = (rest * lower + part * upper) - measured[k]
        field[k : k + 1, :] = jnp.sum(resid * (upper - lower), axis=0, keepdims=True)
        grad[at] = grad[at] + rest * resid
        grad[at + 1] = grad[at + 1] + part * resid
    center_o[...] = grad[pl.ds(at_o, HALO)]
    center_e[...] = grad[pl.ds(at_e, HALO)]
    out_o[0:HALO] = grad[pl.ds(edge_o, HALO)]
    out_e[0:HALO] = grad[pl.ds(edge_e, HALO)]
    left = field[0:EDGE, :]
    right = field[cols - EDGE : cols, :]
    for out, edge in (
        (out_o, jnp.where(odd == 1, right, left)),
        (out_e, jnp.where(odd == 1, left, right)),
    ):
        out[HALO] = jnp.zeros((angles, width), F32)
        out[HALO, 0:EDGE, :] = edge


def land_first(center, landed, weights, out):
    out[0:HALO] = center[...] + landed[0:HALO]
    out[HALO] = weights[0]


def land_second(place, center, landed, other, field, out, wide):
    out[...] = center[...] + landed[0:HALO]
    cols = field.shape[0]
    near, far = landed[HALO, 0:EDGE, :], other[HALO, 0:EDGE, :]
    odd = place[3] == 1
    wide[0:EDGE] = jnp.where(odd, far, near)
    wide[EDGE : EDGE + cols] = field[...]
    wide[EDGE + cols : cols + 2 * EDGE] = jnp.where(odd, near, far)
    wide[cols + 2 * EDGE :] = jnp.zeros((wide.shape[0] - cols - 2 * EDGE, wide.shape[1]), F32)


def spread(place, own_weights, other_weights, own, other, out):
    depth = out.shape[2]
    first = place[1] == 0

    def order(a, b):
        return jnp.concatenate([jnp.where(first, a, b), jnp.where(first, b, a)], axis=0)

    weights = order(own_weights, other_weights).T
    for k in range(0, HALO, 2):
        pair = jnp.concatenate([order(own[k], other[k]), order(own[k + 1], other[k + 1])], axis=1)
        value = jnp.dot(weights, pair, precision=HIGH, preferred_element_type=F32)
        for chunk in range(out.shape[0]):
            rows = value[chunk * depth : (chunk + 1) * depth]
            out[chunk, k] = rows[:, :LANES]
            out[chunk, k + 1] = rows[:, LANES:]


def spread_first(place, own, other, out):
    spread(place, own[HALO], other[HALO], own, other, out)


def spread_second(place, own_e, other_e, own, other, wide, out):
    depth = out.shape[2]
    spread(place, own_e[HALO], other_e[HALO], own, other, out)
    for chunk in range(out.shape[0]):
        out[chunk, HALO] = wide[0:depth]
        out[chunk, HALO + 1] = wide[depth:]


def store(parts, image, base, block, sems):
    chunks, _, _, width = parts.shape
    copies = []
    for k in range(HALO // 8):
        for chunk in range(chunks):
            block[k, :, :, chunk * width : (chunk + 1) * width] = jnp.swapaxes(
                parts[chunk, 8 * k : 8 * k + 8], 0, 1
            )
        columns = pl.ds(pl.multiple_of(base + 8 * k, 8), 8)
        copies.append(pltpu.make_async_copy(block.at[k], image.at[:, columns, :], sems.at[k]))
        copies[k].start()
    return copies


def finish_first(place, parts, image, block, sems):
    for copy in store(parts, image, HALO * (1 - place[3]), block, sems):
        copy.wait()


def finish_second(last, place, parts, partial, image, field, block, sems):
    del partial
    copies = store(parts, image, HALO * place[3], block, sems)
    cols = field.shape[1]
    wide = jnp.concatenate(
        [
            jnp.concatenate([parts[c, HALO], parts[c, HALO + 1]], axis=0)
            for c in range(parts.shape[0])
        ],
        axis=1,
    )[: cols + 2 * EDGE]
    height, total = wide.shape
    row = lax.broadcasted_iota(jnp.int32, wide.shape, 0)
    lane = lax.broadcasted_iota(jnp.int32, wide.shape, 1)
    outside = ((row < EDGE) & (place[2] == 0)) | ((row >= EDGE + cols) & (place[2] == last))
    for _ in range(ITS):
        after = pltpu.roll(wide, height - 1, 0)
        before = pltpu.roll(wide, 1, 0)
        right = jnp.where(lane == total - 1, 0.0, pltpu.roll(wide, total - 1, 1))
        left = jnp.where(lane == 0, 0.0, pltpu.roll(wide, 1, 1))
        laplace = after + before + right + left - 4.0 * wide
        wide = jnp.where(outside, 0.0, wide + DIFFUSION * laplace)
    field[0] = wide[EDGE : EDGE + cols]
    for copy in copies:
        copy.wait()


def body(volume, frac, shift, angle_index, depth_weights, measured):
    depth, cols, height = volume.shape
    angles = angle_index.shape[1]
    slabs, tiles, phases = (lax.axis_size(a) for a in ("slab", "tile", "phase"))
    tile = lax.axis_index("tile")
    place = jnp.stack(
        [lax.axis_index("slab"), lax.axis_index("phase"), tile, tile % 2]
    ).astype(jnp.int32)
    half = (HALO, angles, LANES)
    more = (HALO + 1, angles, LANES)
    halves = pltpu.VMEM((HALO // 8, depth, 8, height), F32)
    two = pltpu.SemaphoreType.DMA((2,))
    pairs_e = [(i, i ^ 1) for i in range(tiles)]
    pairs_o = [(i, ((i + 1) ^ 1) - 1) for i in range(1, tiles - 1)]

    def swap(block, pairs):
        return lax.ppermute(block, "tile", pairs)

    def partner(block):
        return lax.ppermute(block, "phase", [(i, phases - 1 - i) for i in range(phases)])

    def regroup(block):
        return lax.all_to_all(block, "slab", 0, 0, tiled=True)

    parts_o, local = call(
        project_first,
        [(slabs,) + more, (angles, LANES)],
        [SMEM, VMEM, VMEM, ANY],
        [halves, two],
        limit=ROOM,
    )(place, angle_index, depth_weights.T, volume)
    (parts_e,) = call(
        project_second, [(slabs,) + half], [SMEM, VMEM, ANY], [halves, two], limit=ROOM
    )(place, local, volume)
    parts_o = regroup(parts_o)
    parts_o, parts_e = lax.optimization_barrier((parts_o, parts_e))
    parts_e = regroup(parts_e)
    mine, part = call(
        turn,
        [(cols, angles, LANES), (cols, LANES)],
        [SMEM, ANY, ANY],
        [pltpu.VMEM((angles, cols, LANES), F32), two],
        limit=ROOM,
    )(place, measured, frac)
    parts_e, mine, part = lax.optimization_barrier((parts_e, mine, part))
    own_o, weights = call(add_parts, [half, (1, angles, LANES)], [VMEM])(parts_o)
    halo_o = swap(own_o, pairs_o)
    (own_e,) = call(add_parts, [half], [VMEM])(parts_e)
    halo_e = swap(own_e, pairs_e)
    scratch = [pltpu.VMEM((cols + 2 * HALO, angles, LANES), F32)] * 2
    out_o, out_e, center_o, center_e, field = call(
        residual,
        [more, more, half, half, (cols, LANES)],
        [SMEM] * 2 + [VMEM] * 6,
        scratch,
    )(place, shift, own_o, own_e, halo_o, halo_e, mine, part)
    landed_o = swap(out_o, pairs_o)
    landed_e = swap(out_e, pairs_e)
    (adjoint_e,) = call(land_first, [more], [VMEM] * 3)(center_e, landed_e, weights)
    other_e = partner(adjoint_e)
    adjoint_o, wide = call(land_second, [half, (2 * depth, LANES)], [SMEM] + [VMEM] * 4)(
        place, center_o, landed_o, landed_e, field
    )
    other_o = partner(adjoint_o)
    (image_e,) = call(spread_first, [(slabs, HALO, depth, LANES)], [SMEM] + [VMEM] * 2)(
        place, adjoint_e, other_e
    )
    image_e = regroup(image_e)
    (image_o,) = call(spread_second, [(slabs, HALO + 2, depth, LANES)], [SMEM] + [VMEM] * 5)(
        place, adjoint_e, other_e, adjoint_o, other_o, wide
    )
    image_o = regroup(image_o)
    (image,) = call(finish_first, [(depth, cols, height)], [SMEM, VMEM], [halves, two], [ANY])(
        place, image_e
    )

    def ending(*refs):
        finish_second(tiles - 1, *refs)

    return call(
        ending,
        [(depth, cols, height), (1, cols, height)],
        [SMEM, VMEM, ANY],
        [halves, two],
        [ANY, VMEM],
        {2: 0},
    )(place, image_o, image)


def solution(mesh):
    return jax.shard_map(
        body,
        mesh=mesh,
        in_specs=(
            P("slab", "tile", None),
            P("phase", "tile", None),
            P("phase", "tile"),
            P("phase", None),
            P(None, "slab"),
            P("phase", None, "tile", None),
        ),
        out_specs=(P("slab", "tile", None), P("phase", "tile", None)),
        check_vma=False,
    )
```

```python
import jax
import jax.numpy as jnp
from jax import lax
from jax.experimental import pallas as pl
from jax.experimental.pallas import tpu as pltpu
from jax.sharding import PartitionSpec as P

HALO = 16
ITS = 4
DIFFUSION = 0.2
EDGE = 8
REACH = HALO + ITS
LANES = 128
ROOM = 56
HIGH = lax.Precision.HIGHEST
F32 = jnp.float32
VMEM = pl.BlockSpec(memory_space=pltpu.VMEM)
SMEM = pl.BlockSpec(memory_space=pltpu.SMEM)
ANY = pl.BlockSpec(memory_space=pltpu.HBM)


def call(kernel, outs, in_specs, scratch=(), out_specs=None, aliases=None, limit=16):
    return pl.pallas_call(
        kernel,
        out_shape=[jax.ShapeDtypeStruct(o, F32) for o in outs],
        in_specs=in_specs,
        out_specs=out_specs or [VMEM] * len(outs),
        scratch_shapes=list(scratch),
        input_output_aliases=aliases or {},
        compiler_params=pltpu.CompilerParams(vmem_limit_bytes=limit << 20),
        cost_estimate=pl.CostEstimate(flops=1 << 22, bytes_accessed=1 << 21, transcendentals=0),
    )


def outer(a, b):
    return lax.dot_general(
        a, b, (((0,), (0,)), ((), ())), precision=HIGH, preferred_element_type=F32
    )


def project(place, index, table, volume, out, rows, block, staged, sems, done):
    depth, cols, _ = volume.shape
    groups = cols // 8
    entry = pltpu.make_async_copy(table, rows, sems.at[groups])
    entry.start()
    copies = []
    for k in range(groups):
        columns = pl.ds(8 * k, 8)
        copies.append(pltpu.make_async_copy(volume.at[:, columns, :], block.at[k], sems.at[k]))
        copies[k].start()
    entry.wait()
    count = table.shape[1]
    picker = (
        lax.broadcasted_iota(jnp.int32, (count, index.shape[1]), 0) == index[...]
    ).astype(F32)
    flipped = jnp.dot(rows[...], picker, precision=HIGH, preferred_element_type=F32)
    row = lax.broadcasted_iota(jnp.int32, (depth, LANES), 0)
    lane = lax.broadcasted_iota(jnp.int32, (depth, LANES), 1)
    moved = outer(flipped, (lane == row + place[0] * depth).astype(F32))
    weights = outer(flipped, (lane == row).astype(F32))[:, :depth]
    sent = []
    for k in range(groups):
        copies[k].wait()
        turned = jnp.swapaxes(block[k], 0, 1)
        for i in range(8):
            part = jnp.dot(weights, turned[i], precision=HIGH, preferred_element_type=F32)
            for chunk in range(out.shape[0]):
                staged[k, chunk, i] = part[:, chunk * LANES : (chunk + 1) * LANES]
        size = 8
        if k == groups - 1:
            size = 9
            for chunk in range(out.shape[0]):
                staged[k, chunk, 8] = moved
        sent.append(
            pltpu.make_async_copy(
                staged.at[k, :, pl.ds(0, size)], out.at[:, pl.ds(8 * k, size)], done.at[k]
            )
        )
        sent[k].start()
    for copy in sent:
        copy.wait()


def add_parts(place, parts, own, edge_o, edge_e, weights):
    cols = own.shape[0]
    for k in range(cols):
        own[k] = (parts[0, k] + parts[1, k]) + (parts[2, k] + parts[3, k])
    weights[...] = (parts[0, cols] + parts[1, cols]) + (parts[2, cols] + parts[3, cols])
    skip = cols - REACH
    edge_o[...] = own[pl.ds(skip * place[3], REACH)]
    edge_e[...] = own[pl.ds(skip * (1 - place[3]), REACH)]


def turn(place, measured, frac, out, part, edge_o, edge_e, block, sems):
    lanes = pl.ds(pl.multiple_of(place[0] * LANES, LANES), LANES)
    first = pltpu.make_async_copy(measured.at[0, :, :, lanes], block, sems.at[0])
    second = pltpu.make_async_copy(frac.at[0, :, lanes], part, sems.at[1])
    first.start()
    second.start()
    first.wait()
    out[...] = jnp.swapaxes(block[...], 0, 1)
    second.wait()
    for edge, side in ((edge_o, place[3]), (edge_e, 1 - place[3])):
        start = pl.multiple_of(HALO * side, HALO)
        edge[0:HALO] = out[pl.ds(start, HALO)]
        edge[HALO] = jnp.zeros(edge.shape[1:], F32)
        edge[HALO, 0:HALO, :] = part[pl.ds(start, HALO), :]


def residual(
    place, shift, shift_o, shift_e, own, halo_o, halo_e, measured, measured_o, measured_e, frac,
    weights, keep, send, field, ext, seen, share, grad,
):
    odd = place[3]
    cols, angles, width = measured.shape
    ext[REACH : REACH + cols] = own[...]
    ext[pl.ds((REACH + cols) * odd, REACH)] = halo_o[...]
    ext[pl.ds((REACH + cols) * (1 - odd), REACH)] = halo_e[...]
    seen[HALO : HALO + cols] = measured[...]
    share[HALO : HALO + cols, :] = frac[...]
    for ref, side in ((measured_o, odd), (measured_e, 1 - odd)):
        start = pl.multiple_of((HALO + cols) * side, HALO)
        seen[pl.ds(start, HALO)] = ref[0:HALO]
        share[pl.ds(start, HALO), :] = ref[HALO, 0:HALO, :]
    grad[...] = jnp.zeros_like(grad)
    for k in range(cols + 2 * HALO):
        column = k - HALO
        if column < 0:
            step = jnp.where(odd == 1, shift_e[0, cols + column], shift_o[0, cols + column])
        elif column < cols:
            step = shift[0, column]
        else:
            step = jnp.where(odd == 1, shift_o[0, column - cols], shift_e[0, column - cols])
        at = jnp.clip(column + step + REACH, 0, cols + 2 * REACH - 2)
        lower, upper = ext[at], ext[at + 1]
        part = share[k : k + 1, :]
        rest = 1.0 - part
        resid = (rest * lower + part * upper) - seen[k]
        if -EDGE <= column < cols + EDGE:
            value = jnp.sum(resid * (upper - lower), axis=0, keepdims=True)
            for chunk in range(field.shape[0]):
                field[chunk, column + EDGE : column + EDGE + 1, :] = value
        lands = column + step + 2 * HALO
        grad[lands] = grad[lands] + rest * resid
        grad[lands + 1] = grad[lands + 1] + part * resid
    mine = HALO * (2 + place[1])
    theirs = HALO * (3 - place[1])
    keep[...] = grad[pl.ds(mine, HALO)]
    send[0:HALO] = grad[pl.ds(theirs, HALO)]
    send[HALO] = weights[...]


def spread(weights, own, other, out):
    depth = out.shape[2]
    slabs = out.shape[0] // 2
    table = jnp.concatenate([weights[...], other[HALO]], axis=0).T

    def both(k):
        return jnp.concatenate([own[k], other[k]], axis=0)

    for k in range(0, HALO, 2):
        pair = jnp.concatenate([both(k), both(k + 1)], axis=1)
        value = jnp.dot(table, pair, precision=HIGH, preferred_element_type=F32)
        for chunk in range(slabs):
            rows = value[chunk * depth : (chunk + 1) * depth]
            for copy in (chunk, slabs + chunk):
                out[copy, k] = rows[:, :LANES]
                out[copy, k + 1] = rows[:, LANES:]


def diffuse(last, place, parts, field):
    cols = field.shape[1]
    wide = jnp.concatenate([parts[c] for c in range(parts.shape[0])], axis=1)
    height, total = wide.shape
    row = lax.broadcasted_iota(jnp.int32, wide.shape, 0)
    lane = lax.broadcasted_iota(jnp.int32, wide.shape, 1)
    outside = ((row < EDGE) & (place[2] == 0)) | ((row >= EDGE + cols) & (place[2] == last))
    for _ in range(ITS):
        after = pltpu.roll(wide, height - 1, 0)
        before = pltpu.roll(wide, 1, 0)
        right = jnp.where(lane == total - 1, 0.0, pltpu.roll(wide, total - 1, 1))
        left = jnp.where(lane == 0, 0.0, pltpu.roll(wide, 1, 1))
        laplace = after + before + right + left - 4.0 * wide
        wide = jnp.where(outside, 0.0, wide + DIFFUSION * laplace)
    field[0] = wide[EDGE : EDGE + cols]


def finish(parts, image, block, sems):
    slabs = parts.shape[0] // 2
    copies = []
    for k in range(image.shape[1] // 8):
        phase, start = divmod(8 * k, HALO)
        for chunk in range(slabs):
            block[k, :, :, chunk * LANES : (chunk + 1) * LANES] = jnp.swapaxes(
                parts[phase * slabs + chunk, start : start + 8], 0, 1
            )
        columns = pl.ds(8 * k, 8)
        copies.append(pltpu.make_async_copy(block.at[k], image.at[:, columns, :], sems.at[k]))
        copies[k].start()
    for copy in copies:
        copy.wait()


def body(volume, frac, shift, angle_index, depth_weights, measured):
    depth, cols, height = volume.shape
    angles = angle_index.shape[1]
    slabs, tiles, phases = (lax.axis_size(a) for a in ("slab", "tile", "phase"))
    tile = lax.axis_index("tile")
    place = jnp.stack(
        [lax.axis_index("slab"), lax.axis_index("phase"), tile, tile % 2]
    ).astype(jnp.int32)
    half = (HALO, angles, LANES)
    more = (HALO + 1, angles, LANES)
    whole = (cols, angles, LANES)
    edge = (REACH, angles, LANES)
    groups = cols // 8
    blocks = pltpu.VMEM((groups, depth, 8, height), F32)
    dma = pltpu.SemaphoreType.DMA
    pairs_e = [(i, i ^ 1) for i in range(tiles)]
    pairs_o = [(i, ((i + 1) ^ 1) - 1) for i in range(1, tiles - 1)]

    def swap_o(block):
        return lax.ppermute(block, "tile", pairs_o)

    def swap_e(block):
        return lax.ppermute(block, "tile", pairs_e)

    (parts,) = call(
        project,
        [(slabs, cols + 1, angles, LANES)],
        [SMEM, VMEM, ANY, ANY],
        [
            pltpu.VMEM(depth_weights.shape[::-1], F32),
            blocks,
            pltpu.VMEM((groups, slabs, 9, angles, LANES), F32),
            dma((groups + 1,)),
            dma((groups,)),
        ],
        [ANY],
        limit=ROOM,
    )(place, angle_index, depth_weights.T, volume)
    parts = lax.all_to_all(parts, "slab", 0, 0, tiled=True)
    mine, part, edge_o, edge_e = call(
        turn,
        [whole, (cols, LANES), more, more],
        [SMEM, ANY, ANY],
        [pltpu.VMEM((angles, cols, LANES), F32), dma((2,))],
        limit=ROOM,
    )(place, measured, frac)
    measured_o, measured_e = swap_o(edge_o), swap_e(edge_e)
    shift_o, shift_e = swap_o(shift), swap_e(shift)
    parts, mine, part, measured_o, measured_e, shift_o, shift_e = lax.optimization_barrier(
        (parts, mine, part, measured_o, measured_e, shift_o, shift_e)
    )
    own, edge_o, edge_e, weights = call(
        add_parts, [whole, edge, edge, (angles, LANES)], [SMEM, VMEM]
    )(place, parts)
    halo_o, halo_e = swap_o(edge_o), swap_e(edge_e)
    keep, send, field = call(
        residual,
        [half, more, (slabs, cols + 2 * EDGE, LANES)],
        [SMEM] * 4 + [VMEM] * 8,
        [
            pltpu.VMEM((cols + 2 * REACH, angles, LANES), F32),
            pltpu.VMEM((cols + 2 * HALO, angles, LANES), F32),
            pltpu.VMEM((cols + 2 * HALO, LANES), F32),
            pltpu.VMEM((cols + 4 * HALO, angles, LANES), F32),
        ],
    )(
        place, shift, shift_o, shift_e, own, halo_o, halo_e, mine, measured_o, measured_e, part,
        weights,
    )
    other = lax.ppermute(send, "phase", [(i, phases - 1 - i) for i in range(phases)])
    field = lax.all_to_all(field, "slab", 0, 0, tiled=True)
    (parts,) = call(spread, [(phases * slabs, HALO, depth, LANES)], [VMEM] * 3)(
        weights, keep, other
    )
    parts = lax.all_to_all(parts, ("phase", "slab"), 0, 0, tiled=True)

    def steps(*refs):
        diffuse(tiles - 1, *refs)

    (field,) = call(steps, [(1, cols, height)], [SMEM, VMEM])(place, field)
    (image,) = call(
        finish, [(depth, cols, height)], [VMEM], [blocks, dma((groups,))], [ANY]
    )(parts)
    return image, field


def solution(mesh):
    return jax.shard_map(
        body,
        mesh=mesh,
        in_specs=(
            P("slab", "tile", None),
            P("phase", "tile", None),
            P("phase", "tile"),
            P("phase", None),
            P(None, "slab"),
            P("phase", None, "tile", None),
        ),
        out_specs=(P("slab", "tile", None), P("phase", "tile", None)),
        check_vma=False,
    )
```

```python
import jax
import jax.numpy as jnp
from jax import lax
from jax.experimental import pallas as pl
from jax.experimental.pallas import tpu as pltpu
from jax.sharding import PartitionSpec as P

HALO = 16
ITS = 4
DIFFUSION = 0.2
EDGE = 8
SPAN = 3 * HALO
ROWS = 24
LANES = 128
ROOM = 56
HIGH = lax.Precision.HIGHEST
F32 = jnp.float32
VMEM = pl.BlockSpec(memory_space=pltpu.VMEM)
SMEM = pl.BlockSpec(memory_space=pltpu.SMEM)
ANY = pl.BlockSpec(memory_space=pltpu.HBM)


def call(kernel, outs, in_specs, scratch=(), out_specs=None, aliases=None, limit=16):
    return pl.pallas_call(
        kernel,
        out_shape=[jax.ShapeDtypeStruct(o, F32) for o in outs],
        in_specs=in_specs,
        out_specs=out_specs or [VMEM] * len(outs),
        scratch_shapes=list(scratch),
        input_output_aliases=aliases or {},
        compiler_params=pltpu.CompilerParams(vmem_limit_bytes=limit << 20),
        cost_estimate=pl.CostEstimate(flops=1 << 22, bytes_accessed=1 << 21, transcendentals=0),
    )


def outer(a, b):
    return lax.dot_general(
        a, b, (((0,), (0,)), ((), ())), precision=HIGH, preferred_element_type=F32
    )


def rim(place, volume, out, block, sem):
    cols = volume.shape[1]
    start = pl.multiple_of((cols - 8) * (1 - place[1]), 8)
    copy = pltpu.make_async_copy(volume.at[:, pl.ds(start, 8), :], block, sem.at[0])
    copy.start()
    copy.wait()
    out[...] = jnp.where(place[1] == 0, block[:, 7, :], block[:, 0, :])


def bundle(place, shift, measured, frac, whole, same, cross, sems):
    angles, cols = measured.shape[1:3]
    lanes = pl.ds(pl.multiple_of(place[0] * LANES, LANES), LANES)
    first = pltpu.make_async_copy(measured.at[0, :, :, lanes], whole.at[pl.ds(0, angles)], sems.at[0])
    second = pltpu.make_async_copy(frac.at[0, :, lanes], whole.at[angles], sems.at[1])
    first.start()
    second.start()
    for k in range(cols):
        value = jnp.full((1, LANES), shift[0, k], jnp.int32).astype(F32)
        whole[angles + 1, k : k + 1, :] = value
    first.wait()
    second.wait()
    here = pl.multiple_of(HALO * (1 - place[1]), HALO)
    there = pl.multiple_of(HALO * place[1], HALO)
    same[...] = whole[:, pl.ds(here, HALO), :]
    cross[...] = whole[:, pl.ds(there, HALO), :]


def cut(place, volume, out, block, staged, sems, done):
    copies, sent = [], []
    for k in range(HALO // 8):
        columns = pl.ds(pl.multiple_of(HALO * place[1] + 8 * k, 8), 8)
        copies.append(pltpu.make_async_copy(volume.at[:, columns, :], block.at[k], sems.at[k]))
        copies[k].start()
    for k, copy in enumerate(copies):
        copy.wait()
        turned = jnp.swapaxes(block[k], 0, 1)
        for chunk in range(out.shape[0]):
            staged[k, chunk] = turned[:, :, chunk * LANES : (chunk + 1) * LANES]
        sent.append(pltpu.make_async_copy(staged.at[k], out.at[:, pl.ds(8 * k, 8)], done.at[k]))
        sent[k].start()
    for copy in sent:
        copy.wait()


def pack(place, index, other, table, volume, beside, out, block, sem):
    depth, cols, _ = volume.shape
    start = pl.multiple_of(HALO - 8 * place[1], 8)
    copy = pltpu.make_async_copy(volume.at[:, pl.ds(start, 8), :], block, sem.at[0])
    copy.start()
    row = lax.broadcasted_iota(jnp.int32, (depth, LANES), 0)
    lane = lax.broadcasted_iota(jnp.int32, (depth, LANES), 1)
    number = lax.broadcasted_iota(jnp.int32, (table.shape[1], index.shape[1]), 0)
    slabs = out.shape[0]
    for k, name in enumerate((index, other)):
        picker = (number == name[...]).astype(F32)
        flipped = jnp.dot(table[...], picker, precision=HIGH, preferred_element_type=F32)
        weights = outer(flipped, (lane == row + place[0] * depth).astype(F32))
        for chunk in range(slabs):
            out[chunk, k] = weights
    copy.wait()
    first = place[1] == 0
    inner = jnp.where(first, block[:, 0, :], block[:, 7, :])
    low = jnp.where(first, beside[...], inner)
    high = jnp.where(first, inner, beside[...])
    for chunk in range(slabs):
        lanes = slice(chunk * LANES, (chunk + 1) * LANES)
        out[chunk, 2] = low[:, lanes]
        out[chunk, 3] = high[:, lanes]


def split(place, made, *outs):
    slabs = made.shape[0]
    for k, out in enumerate(outs):
        to = place[0] + k
        out[...] = made[jnp.where(to >= slabs, to - slabs, to)]


def arrange(place, own, other, same, cross, seen, share, steps):
    phase = place[1]
    angles = own.shape[0] - 2
    middle = pl.multiple_of(HALO * (1 - phase), HALO)
    side = pl.multiple_of(2 * HALO * phase, HALO)
    for to, inside, beyond in ((phase, own, same), (1 - phase, other, cross)):
        for ref, start in ((inside, middle), (beyond, side)):
            size = ref.shape[1]
            seen[to, pl.ds(start, size)] = jnp.swapaxes(ref[0:angles], 0, 1)
            share[to, pl.ds(start, size), :] = ref[angles]
            steps[to, pl.ds(start, size), :] = ref[angles + 1]


def core(
    place, steps, parts, a, b, c, d, seen, share, out, kept, crossed, down, down_x, up, up_x,
    ext, grad, field, canvas, beside,
):
    slabs, half, depth, width = parts.shape
    angles = seen.shape[2]
    phase = place[1]

    mine, theirs = ((a[k] + b[k]) + (c[k] + d[k]) for k in range(2))
    weights = jnp.concatenate(
        [jnp.where(phase == 0, mine, theirs), jnp.where(phase == 0, theirs, mine)], axis=0
    )
    for k, ref in enumerate((a, b, c, d)):
        source = place[0] - k
        source = jnp.where(source < 0, source + slabs, source)
        rows = pl.ds(pl.multiple_of(source * depth, depth), depth)
        beside[0, rows, :] = ref[2]
        beside[1, rows, :] = ref[3]
    nothing = jnp.zeros((2 * angles, width), F32)

    def put(columns, at):
        value = jnp.concatenate(columns, axis=1)
        value = jnp.dot(weights, value, precision=HIGH, preferred_element_type=F32)
        for k in range(len(columns)):
            ext[at[k]] = value[:, k * width : (k + 1) * width]

    for k in range(0, half, 2):
        columns = [
            jnp.concatenate([parts[s, k + i] for s in range(slabs)], axis=0) for i in range(2)
        ]
        put(columns, (k + 2, k + 3))
    put([beside[0], beside[1]], (1, half + 2))
    ext[0] = nothing
    ext[half + 3] = nothing
    grad[...] = jnp.zeros_like(grad)
    field[...] = jnp.zeros_like(field)
    outermost = jnp.where((phase == 0) & (place[2] == 0), 1, 2)
    for q in range(2):
        rows = slice(q * angles, (q + 1) * angles)
        for j in range(seen.shape[1]):
            at = j + steps[q, j] - 14

            @pl.when((at >= 1) & (at <= half + 1))
            def _(q=q, j=j, at=at, rows=rows):
                lower, upper = ext[at, rows, :], ext[at + 1, rows, :]
                part = share[q, j : j + 1, :]
                rest = 1.0 - part
                resid = (rest * lower + part * upper) - seen[q, j]
                value = jnp.sum(resid * (upper - lower), axis=0, keepdims=True)
                field[q, j : j + 1, :] = jnp.where(at >= outermost, value, 0.0)
                grad[at, rows, :] = grad[at, rows, :] + rest * resid
                grad[at + 1, rows, :] = grad[at + 1, rows, :] + part * resid

    table = weights.T
    for k in range(0, half, 2):
        pair = jnp.concatenate([grad[k + 2], grad[k + 3]], axis=1)
        value = jnp.dot(table, pair, precision=HIGH, preferred_element_type=F32)
        for chunk in range(slabs):
            part = value[chunk * depth : (chunk + 1) * depth]
            for copy in (chunk, slabs + chunk):
                out[copy, k] = part[:, :width]
                out[copy, k + 1] = part[:, width:]
    canvas[...] = jnp.zeros_like(canvas)
    start = pl.multiple_of(HALO * phase, HALO)
    for q in range(2):
        canvas[q, pl.ds(start, seen.shape[1]), :] = field[q]
    for q, (home, left, right) in ((phase, (kept, down, up)), (1 - phase, (crossed, down_x, up_x))):
        home[...] = canvas[q, EDGE : EDGE + SPAN, :]
        left[...] = canvas[q, 0:ROWS, :]
        right[...] = canvas[q, canvas.shape[1] - ROWS :, :]


def collect(kept, crossed, left, left_x, right, right_x, out):
    total = kept[...] + crossed[...]
    out[0:ROWS, :] = total[0:ROWS] + (left[...] + left_x[...])
    out[ROWS:, :] = total[ROWS:] + (right[...] + right_x[...])


def diffuse(last, place, a, b, c, d, field, chunks):
    cols = field.shape[1]
    for k, ref in enumerate((a, b, c, d)):
        source = place[0] - k
        chunks[jnp.where(source < 0, source + 4, source)] = ref[...]
    wide = jnp.concatenate([chunks[k] for k in range(chunks.shape[0])], axis=1)
    height, total = wide.shape
    row = lax.broadcasted_iota(jnp.int32, wide.shape, 0)
    lane = lax.broadcasted_iota(jnp.int32, wide.shape, 1)
    outside = ((row < EDGE) & (place[2] == 0)) | ((row >= EDGE + cols) & (place[2] == last))
    for _ in range(ITS):
        after = pltpu.roll(wide, height - 1, 0)
        before = pltpu.roll(wide, 1, 0)
        right = jnp.where(lane == total - 1, 0.0, pltpu.roll(wide, total - 1, 1))
        left = jnp.where(lane == 0, 0.0, pltpu.roll(wide, 1, 1))
        laplace = after + before + right + left - 4.0 * wide
        wide = jnp.where(outside, 0.0, wide + DIFFUSION * laplace)
    field[0] = wide[EDGE : EDGE + cols]


def finish(parts, image, block, sems):
    slabs = parts.shape[0] // 2
    copies = []
    for k in range(image.shape[1] // 8):
        phase, start = divmod(8 * k, HALO)
        for chunk in range(slabs):
            block[k, :, :, chunk * LANES : (chunk + 1) * LANES] = jnp.swapaxes(
                parts[phase * slabs + chunk, start : start + 8], 0, 1
            )
        columns = pl.ds(8 * k, 8)
        copies.append(pltpu.make_async_copy(block.at[k], image.at[:, columns, :], sems.at[k]))
        copies[k].start()
    for copy in copies:
        copy.wait()


def move(block, target):
    phases, tiles = lax.axis_size("phase"), lax.axis_size("tile")
    route = []
    for phase in range(phases):
        for tile in range(tiles):
            to_phase, to_tile = target(phase, tile)
            if 0 <= to_tile < tiles:
                route.append((phase * tiles + tile, to_phase * tiles + to_tile))
    return lax.ppermute(block, ("phase", "tile"), route)


def body(volume, frac, shift, angle_index, depth_weights, measured):
    depth, cols, height = volume.shape
    angles = angle_index.shape[1]
    slabs, tiles, phases = (lax.axis_size(a) for a in ("slab", "tile", "phase"))
    group = phases * slabs
    place = jnp.stack(
        [lax.axis_index("slab"), lax.axis_index("phase"), lax.axis_index("tile")]
    ).astype(jnp.int32)
    octet = pltpu.VMEM((depth, 8, height), F32)
    blocks = pltpu.VMEM((cols // 8, depth, 8, height), F32)
    dma = pltpu.SemaphoreType.DMA

    def toward(phase, tile):
        return phase, tile + 1 - 2 * phase

    def across(phase, tile):
        return 1 - phase, tile - 1 + 2 * phase

    def partner(phase, tile):
        return 1 - phase, tile

    def around(block, distance):
        return lax.ppermute(block, "slab", [(i, (i + distance) % slabs) for i in range(slabs)])

    (edge,) = call(rim, [(depth, height)], [SMEM, ANY], [octet, dma((1,))], limit=ROOM)(
        place, volume
    )
    beside = move(edge, toward)
    index_other = move(angle_index, partner)
    bundles = [(angles + 2, cols, LANES)] + [(angles + 2, HALO, LANES)] * 2
    bundle_own, same, cross = call(
        bundle, bundles, [SMEM] * 2 + [ANY] * 2, [dma((2,))], limit=ROOM
    )(place, shift, measured, frac)
    bundle_other = move(bundle_own, partner)
    (parts,) = call(
        cut,
        [(slabs, HALO, depth, LANES)],
        [SMEM, ANY],
        [
            pltpu.VMEM((HALO // 8, depth, 8, height), F32),
            pltpu.VMEM((HALO // 8, slabs, 8, depth, LANES), F32),
            dma((HALO // 8,)),
            dma((HALO // 8,)),
        ],
        [ANY],
        limit=ROOM,
    )(place, volume)
    parts = lax.all_to_all(parts, "slab", 0, 0, tiled=True)
    same = move(same, toward)
    cross = move(cross, across)
    (extra,) = call(
        pack, [(slabs, 4, depth, LANES)], [SMEM, VMEM, VMEM, VMEM, ANY, VMEM], [octet, dma((1,))],
        limit=ROOM,
    )(place, angle_index, index_other, depth_weights.T, volume, beside)
    extras = call(split, [(4, depth, LANES)] * slabs, [SMEM, VMEM])(place, extra)
    extras = [extras[0]] + [around(extras[k], k) for k in range(1, slabs)]
    seen, share, steps = call(
        arrange,
        [(phases, SPAN, angles, LANES), (phases, SPAN, LANES), (phases, SPAN, LANES)],
        [SMEM] + [VMEM] * 4,
    )(place, bundle_own, bundle_other, same, cross)
    steps = steps[:, :, 0].astype(jnp.int32)
    parts, seen, share, steps, *extras = lax.optimization_barrier(
        (parts, seen, share, steps, *extras)
    )
    window, side = (SPAN, LANES), (ROWS, LANES)
    stack = (HALO + 4, 2 * angles, LANES)
    parts, kept, crossed, down, down_x, up, up_x = call(
        core,
        [(group, HALO, depth, LANES), window, window, side, side, side, side],
        [SMEM] * 2 + [VMEM] * 7,
        [
            pltpu.VMEM(stack, F32),
            pltpu.VMEM(stack, F32),
            pltpu.VMEM((phases, SPAN, LANES), F32),
            pltpu.VMEM((phases, 4 * HALO, LANES), F32),
            pltpu.VMEM((2, slabs * depth, LANES), F32),
        ],
    )(place, steps, parts, *extras, seen, share)
    parts = lax.all_to_all(parts, ("phase", "slab"), 0, 0, tiled=True)
    (field,) = call(collect, [window], [VMEM] * 6)(
        kept,
        move(crossed, partner),
        move(up, lambda phase, tile: (phase, tile + 1)),
        move(up_x, lambda phase, tile: (1 - phase, tile + 1)),
        move(down, lambda phase, tile: (phase, tile - 1)),
        move(down_x, lambda phase, tile: (1 - phase, tile - 1)),
    )
    fields = [field] + [around(field, k) for k in range(1, slabs)]

    def ending(*refs):
        diffuse(tiles - 1, *refs)

    (field,) = call(
        ending,
        [(1, cols, height)],
        [SMEM] + [VMEM] * 4,
        [pltpu.VMEM((slabs,) + window, F32)],
    )(place, *fields)
    (image,) = call(
        finish, [(depth, cols, height)], [VMEM], [blocks, dma((cols // 8,))], [ANY]
    )(parts)
    return image, field


def solution(mesh):
    return jax.shard_map(
        body,
        mesh=mesh,
        in_specs=(
            P("slab", "tile", None),
            P("phase", "tile", None),
            P("phase", "tile"),
            P("phase", None),
            P(None, "slab"),
            P("phase", None, "tile", None),
        ),
        out_specs=(P("slab", "tile", None), P("phase", "tile", None)),
        check_vma=False,
    )
```

```python
import jax
import jax.numpy as jnp
from jax import lax
from jax.experimental import pallas as pl
from jax.experimental.pallas import tpu as pltpu
from jax.sharding import PartitionSpec as P

HALO = 16
ITS = 4
DIFFUSION = 0.2
EDGE = 8
SPAN = 3 * HALO
ROWS = 24
LANES = 128
ROOM = 56
HIGH = lax.Precision.HIGHEST
F32 = jnp.float32
VMEM = pl.BlockSpec(memory_space=pltpu.VMEM)
SMEM = pl.BlockSpec(memory_space=pltpu.SMEM)
ANY = pl.BlockSpec(memory_space=pltpu.HBM)


def call(kernel, outs, in_specs, scratch=(), out_specs=None, aliases=None, limit=16):
    return pl.pallas_call(
        kernel,
        out_shape=[jax.ShapeDtypeStruct(o, F32) for o in outs],
        in_specs=in_specs,
        out_specs=out_specs or [VMEM] * len(outs),
        scratch_shapes=list(scratch),
        input_output_aliases=aliases or {},
        compiler_params=pltpu.CompilerParams(vmem_limit_bytes=limit << 20),
        cost_estimate=pl.CostEstimate(flops=1 << 22, bytes_accessed=1 << 21, transcendentals=0),
    )


def outer(a, b):
    return lax.dot_general(
        a, b, (((0,), (0,)), ((), ())), precision=HIGH, preferred_element_type=F32
    )


def load(
    place, shift, measured, frac, volume, whole, same, cross, rim, parts, block, half, sems, done
):
    angles, cols = measured.shape[1:3]
    phase = place[1]
    copies = []

    def start(source, target):
        copies.append(pltpu.make_async_copy(source, target, sems.at[len(copies)]))
        copies[-1].start()

    columns = pl.ds(pl.multiple_of(HALO * phase, HALO), HALO)
    slabs = parts.shape[0]
    for k in range(slabs):
        start(volume.at[:, columns, pl.ds(k * LANES, LANES)], half.at[k])
    edge = pl.multiple_of((cols - 8) * (1 - phase), 8)
    start(volume.at[:, pl.ds(edge, 8), :], block)
    lanes = pl.ds(pl.multiple_of(place[0] * LANES, LANES), LANES)
    start(measured.at[0, :, :, lanes], whole.at[pl.ds(0, angles)])
    start(frac.at[0, :, lanes], whole.at[angles])
    for k in range(cols):
        whole[angles + 1, k : k + 1, :] = jnp.full((1, LANES), shift[0, k], jnp.int32).astype(F32)
    sent = []
    for k in range(slabs):
        copies[k].wait()
        sent.append(pltpu.make_async_copy(half.at[k], parts.at[k], done.at[k]))
        sent[k].start()
    for copy in copies[slabs:]:
        copy.wait()
    rim[...] = jnp.where(phase == 0, block[:, 7, :], block[:, 0, :])
    same[...] = whole[:, pl.ds(pl.multiple_of(HALO * (1 - phase), HALO), HALO), :]
    cross[...] = whole[:, columns, :]
    for copy in sent:
        copy.wait()


def pack(place, index, other, rim, table, volume, first, second, third, fourth, block, low, high, sem):
    depth, cols, _ = volume.shape
    angles = index.shape[1]
    start = pl.multiple_of(HALO - 8 * place[1], 8)
    copy = pltpu.make_async_copy(volume.at[:, pl.ds(start, 8), :], block, sem.at[0])
    copy.start()
    numbers = jnp.concatenate([index[...], other[...]], axis=1)
    count = table.shape[1]
    picker = (lax.broadcasted_iota(jnp.int32, (count, 2 * angles), 0) == numbers).astype(F32)
    flipped = jnp.dot(table[...], picker, precision=HIGH, preferred_element_type=F32)
    row = lax.broadcasted_iota(jnp.int32, (depth, LANES), 0)
    lane = lax.broadcasted_iota(jnp.int32, (depth, LANES), 1)
    weights = outer(flipped, (lane == row + place[0] * depth).astype(F32))
    left = place[1] == 0
    beside = rim[...]
    copy.wait()
    inner = jnp.where(left, block[:, 0, :], block[:, 7, :])
    low[...] = jnp.where(left, beside, inner)
    high[...] = jnp.where(left, inner, beside)
    slabs = volume.shape[2] // LANES
    for k, out in enumerate((first, second, third, fourth)):
        to = place[0] + k
        to = jnp.where(to >= slabs, to - slabs, to)
        lanes = pl.ds(pl.multiple_of(to * LANES, LANES), LANES)
        out[0] = weights[0:angles]
        out[1] = weights[angles:]
        out[2] = low[:, lanes]
        out[3] = high[:, lanes]


def arrange(place, own, other, same, cross, seen, share, steps):
    phase = place[1]
    angles = own.shape[0] - 2
    middle = pl.multiple_of(HALO * (1 - phase), HALO)
    side = pl.multiple_of(2 * HALO * phase, HALO)
    for to, inside, beyond in ((phase, own, same), (1 - phase, other, cross)):
        for ref, start in ((inside, middle), (beyond, side)):
            size = ref.shape[1]
            seen[to, pl.ds(start, size)] = jnp.swapaxes(ref[0:angles], 0, 1)
            share[to, pl.ds(start, size), :] = ref[angles]
            steps[to, pl.ds(start, size), :] = ref[angles + 1]


def core(
    place, steps, parts, a, b, c, d, seen, share, grad, weights, own, other,
    ext, field, canvas, beside,
):
    slabs, depth, half, width = parts.shape
    angles = seen.shape[2]
    phase = place[1]
    mine, theirs = ((a[k] + b[k]) + (c[k] + d[k]) for k in range(2))
    table = jnp.concatenate(
        [jnp.where(phase == 0, mine, theirs), jnp.where(phase == 0, theirs, mine)], axis=0
    )
    weights[...] = table
    for k, ref in enumerate((a, b, c, d)):
        source = place[0] - k
        source = jnp.where(source < 0, source + slabs, source)
        rows = pl.ds(pl.multiple_of(source * depth, depth), depth)
        beside[0, rows, :] = ref[2]
        beside[1, rows, :] = ref[3]
    nothing = jnp.zeros((2 * angles, width), F32)

    def put(columns, at):
        value = jnp.concatenate(columns, axis=1)
        value = jnp.dot(table, value, precision=HIGH, preferred_element_type=F32)
        for k in range(len(columns)):
            ext[at[k]] = value[:, k * width : (k + 1) * width]

    for base in range(0, half, 8):
        turned = [jnp.swapaxes(parts[s, :, base : base + 8, :], 0, 1) for s in range(slabs)]
        for k in range(0, 8, 2):
            columns = [
                jnp.concatenate([turned[s][k + i] for s in range(slabs)], axis=0)
                for i in range(2)
            ]
            put(columns, (base + k + 2, base + k + 3))
    put([beside[0], beside[1]], (1, half + 2))
    ext[0] = nothing
    ext[half + 3] = nothing
    grad[...] = jnp.zeros_like(grad)
    field[...] = jnp.zeros_like(field)
    outermost = jnp.where((phase == 0) & (place[2] == 0), 1, 2)
    for q in range(2):
        rows = slice(q * angles, (q + 1) * angles)
        for j in range(seen.shape[1]):
            at = j + steps[q, j] - 14

            @pl.when((at >= 1) & (at <= half + 1))
            def _(q=q, j=j, at=at, rows=rows):
                lower, upper = ext[at, rows, :], ext[at + 1, rows, :]
                part = share[q, j : j + 1, :]
                rest = 1.0 - part
                resid = (rest * lower + part * upper) - seen[q, j]
                value = jnp.sum(resid * (upper - lower), axis=0, keepdims=True)
                field[q, j : j + 1, :] = jnp.where(at >= outermost, value, 0.0)
                grad[at, rows, :] = grad[at, rows, :] + rest * resid
                grad[at + 1, rows, :] = grad[at + 1, rows, :] + part * resid

    canvas[...] = jnp.zeros_like(canvas)
    start = pl.multiple_of(HALO * phase, HALO)
    for q in range(2):
        canvas[q, pl.ds(start, seen.shape[1]), :] = field[q]
    own[...] = canvas[phase]
    other[...] = canvas[1 - phase]


def spread(grad, weights, out, staged, sems):
    slabs, half, depth, width = staged.shape
    table = weights[...].T
    copies = []
    for k in range(0, half, 2):
        pair = jnp.concatenate([grad[k + 2], grad[k + 3]], axis=1)
        value = jnp.dot(table, pair, precision=HIGH, preferred_element_type=F32)
        for chunk in range(slabs):
            part = value[chunk * depth : (chunk + 1) * depth]
            staged[chunk, k] = part[:, :width]
            staged[chunk, k + 1] = part[:, width:]
        if k % 4 == 2:
            columns = pl.ds(k - 2, 4)
            for to in range(2):
                target = out.at[pl.ds(to * slabs, slabs), columns]
                copies.append(
                    pltpu.make_async_copy(staged.at[:, columns], target, sems.at[len(copies)])
                )
                copies[-1].start()
    for copy in copies:
        copy.wait()


def merge(place, own, other, kept, side_o, side_e):
    total = own[...] + other[...]
    kept[...] = total[EDGE : EDGE + SPAN]
    left, right = total[0:ROWS], total[total.shape[0] - ROWS :]
    odd = place[3] == 1
    side_o[...] = jnp.where(odd, right, left)
    side_e[...] = jnp.where(odd, left, right)


def collect(place, kept, side_o, side_e, out):
    odd = place[3] == 1
    from_left = jnp.where(odd, side_e[...], side_o[...])
    from_right = jnp.where(odd, side_o[...], side_e[...])
    out[0:ROWS, :] = kept[0:ROWS] + from_left
    out[ROWS:, :] = kept[ROWS:] + from_right


def diffuse(last, place, a, b, c, d, field, chunks):
    cols = field.shape[1]
    for k, ref in enumerate((a, b, c, d)):
        source = place[0] - k
        chunks[jnp.where(source < 0, source + 4, source)] = ref[...]
    wide = jnp.concatenate([chunks[k] for k in range(chunks.shape[0])], axis=1)
    height, total = wide.shape
    row = lax.broadcasted_iota(jnp.int32, wide.shape, 0)
    lane = lax.broadcasted_iota(jnp.int32, wide.shape, 1)
    outside = ((row < EDGE) & (place[2] == 0)) | ((row >= EDGE + cols) & (place[2] == last))
    for _ in range(ITS):
        after = pltpu.roll(wide, height - 1, 0)
        before = pltpu.roll(wide, 1, 0)
        right = jnp.where(lane == total - 1, 0.0, pltpu.roll(wide, total - 1, 1))
        left = jnp.where(lane == 0, 0.0, pltpu.roll(wide, 1, 1))
        laplace = after + before + right + left - 4.0 * wide
        wide = jnp.where(outside, 0.0, wide + DIFFUSION * laplace)
    field[0] = wide[EDGE : EDGE + cols]


def finish(parts, image, block, sems):
    slabs = parts.shape[0] // 2
    copies = []
    for k in range(image.shape[1] // 8):
        phase, start = divmod(8 * k, HALO)
        for chunk in range(slabs):
            block[k, :, :, chunk * LANES : (chunk + 1) * LANES] = jnp.swapaxes(
                parts[phase * slabs + chunk, start : start + 8], 0, 1
            )
        columns = pl.ds(8 * k, 8)
        copies.append(pltpu.make_async_copy(block.at[k], image.at[:, columns, :], sems.at[k]))
        copies[k].start()
    for copy in copies:
        copy.wait()


def move(block, target):
    phases, tiles = lax.axis_size("phase"), lax.axis_size("tile")
    route = []
    for phase in range(phases):
        for tile in range(tiles):
            to_phase, to_tile = target(phase, tile)
            if 0 <= to_tile < tiles:
                route.append((phase * tiles + tile, to_phase * tiles + to_tile))
    return lax.ppermute(block, ("phase", "tile"), route)


def body(volume, frac, shift, angle_index, depth_weights, measured):
    depth, cols, height = volume.shape
    angles = angle_index.shape[1]
    slabs, tiles, phases = (lax.axis_size(a) for a in ("slab", "tile", "phase"))
    group = phases * slabs
    tile = lax.axis_index("tile")
    place = jnp.stack(
        [lax.axis_index("slab"), lax.axis_index("phase"), tile, tile % 2]
    ).astype(jnp.int32)
    octet = pltpu.VMEM((depth, 8, height), F32)
    blocks = pltpu.VMEM((cols // 8, depth, 8, height), F32)
    dma = pltpu.SemaphoreType.DMA

    def toward(phase, tile):
        return phase, tile + 1 - 2 * phase

    def across(phase, tile):
        return 1 - phase, tile - 1 + 2 * phase

    def partner(phase, tile):
        return 1 - phase, tile

    def around(block, distance):
        return lax.ppermute(block, "slab", [(i, (i + distance) % slabs) for i in range(slabs)])

    bundles = [(angles + 2, cols, LANES)] + [(angles + 2, HALO, LANES)] * 2
    message = (slabs, depth, HALO, LANES)
    bundle_own, same, cross, rim, parts = call(
        load,
        bundles + [(depth, height), message],
        [SMEM] * 2 + [ANY] * 3,
        [octet, pltpu.VMEM(message, F32), dma((slabs + 3,)), dma((slabs,))],
        [VMEM] * 4 + [ANY],
        limit=ROOM,
    )(place, shift, measured, frac, volume)
    rim = move(rim, toward)
    index_other = move(angle_index, partner)
    bundle_other = move(bundle_own, partner)
    parts, index_other = lax.optimization_barrier((parts, index_other))
    parts = lax.all_to_all(parts, "slab", 0, 0, tiled=True)
    same = move(same, toward)
    cross = move(cross, across)
    wide = pltpu.VMEM((depth, height), F32)
    extras = call(
        pack,
        [(4, depth, LANES)] * slabs,
        [SMEM] + [VMEM] * 4 + [ANY],
        [octet, wide, wide, dma((1,))],
    )(place, angle_index, index_other, rim, depth_weights.T, volume)
    extras = [extras[0]] + [around(extras[k], k) for k in range(1, slabs)]
    seen, share, steps = call(
        arrange,
        [(phases, SPAN, angles, LANES), (phases, SPAN, LANES), (phases, SPAN, LANES)],
        [SMEM] + [VMEM] * 4,
    )(place, bundle_own, bundle_other, same, cross)
    steps = steps[:, :, 0].astype(jnp.int32)
    parts, seen, share, steps, *extras = lax.optimization_barrier(
        (parts, seen, share, steps, *extras)
    )
    window, side, canvas = (SPAN, LANES), (ROWS, LANES), (4 * HALO, LANES)
    stack = (HALO + 4, 2 * angles, LANES)
    grad, weights, own, other = call(
        core,
        [stack, (2 * angles, LANES), canvas, canvas],
        [SMEM] * 2 + [VMEM] * 7,
        [
            pltpu.VMEM(stack, F32),
            pltpu.VMEM((phases, SPAN, LANES), F32),
            pltpu.VMEM((phases,) + canvas, F32),
            pltpu.VMEM((2, slabs * depth, LANES), F32),
        ],
    )(place, steps, parts, *extras, seen, share)
    (parts,) = call(
        spread,
        [(group, HALO, depth, LANES)],
        [VMEM] * 2,
        [pltpu.VMEM((slabs, HALO, depth, LANES), F32), dma((HALO // 2,))],
        [ANY],
        limit=ROOM,
    )(grad, weights)
    other = move(other, partner)
    parts, other = lax.optimization_barrier((parts, other))
    parts = lax.all_to_all(parts, ("phase", "slab"), 0, 0, tiled=True)
    kept, side_o, side_e = call(merge, [window, side, side], [SMEM] + [VMEM] * 2)(
        place, own, other
    )
    pairs_e = [(i, i ^ 1) for i in range(tiles)]
    pairs_o = [(i, ((i + 1) ^ 1) - 1) for i in range(1, tiles - 1)]
    (field,) = call(collect, [window], [SMEM] + [VMEM] * 3)(
        place, kept, lax.ppermute(side_o, "tile", pairs_o), lax.ppermute(side_e, "tile", pairs_e)
    )
    fields = [field] + [around(field, k) for k in range(1, slabs)]

    def ending(*refs):
        diffuse(tiles - 1, *refs)

    (field,) = call(
        ending,
        [(1, cols, height)],
        [SMEM] + [VMEM] * 4,
        [pltpu.VMEM((slabs,) + window, F32)],
    )(place, *fields)
    (image,) = call(
        finish, [(depth, cols, height)], [VMEM], [blocks, dma((cols // 8,))], [ANY]
    )(parts)
    return image, field


def solution(mesh):
    return jax.shard_map(
        body,
        mesh=mesh,
        in_specs=(
            P("slab", "tile", None),
            P("phase", "tile", None),
            P("phase", "tile"),
            P("phase", None),
            P(None, "slab"),
            P("phase", None, "tile", None),
        ),
        out_specs=(P("slab", "tile", None), P("phase", "tile", None)),
        check_vma=False,
    )
```

```python
import jax
import jax.numpy as jnp
from jax import lax
from jax.experimental import pallas as pl
from jax.experimental.pallas import tpu as pltpu
from jax.sharding import PartitionSpec as P

HALO = 16
ITS = 4
DIFFUSION = 0.2
EDGE = 8
SPAN = 3 * HALO
ROWS = 24
LANES = 128
ROOM = 56
HIGH = lax.Precision.HIGHEST
F32 = jnp.float32
VMEM = pl.BlockSpec(memory_space=pltpu.VMEM)
SMEM = pl.BlockSpec(memory_space=pltpu.SMEM)
ANY = pl.BlockSpec(memory_space=pltpu.HBM)


def call(kernel, outs, in_specs, scratch=(), out_specs=None, aliases=None, limit=16):
    return pl.pallas_call(
        kernel,
        out_shape=[jax.ShapeDtypeStruct(o, F32) for o in outs],
        in_specs=in_specs,
        out_specs=out_specs or [VMEM] * len(outs),
        scratch_shapes=list(scratch),
        input_output_aliases=aliases or {},
        compiler_params=pltpu.CompilerParams(vmem_limit_bytes=limit << 20),
        cost_estimate=pl.CostEstimate(flops=1 << 22, bytes_accessed=1 << 21, transcendentals=0),
    )


def outer(a, b):
    return lax.dot_general(
        a, b, (((0,), (0,)), ((), ())), precision=HIGH, preferred_element_type=F32
    )


def load(
    place, shift, measured, frac, volume, whole, same, cross, parts, block, half, sems, done
):
    angles, cols = measured.shape[1:3]
    phase = place[1]
    copies = []

    def start(source, target):
        copies.append(pltpu.make_async_copy(source, target, sems.at[len(copies)]))
        copies[-1].start()

    columns = pl.ds(pl.multiple_of(HALO * phase, HALO), HALO)
    slabs = parts.shape[0]
    for k in range(slabs):
        start(volume.at[:, columns, pl.ds(k * LANES, LANES)], half.at[k])
    edge = pl.multiple_of((cols - 8) * (1 - phase), 8)
    start(volume.at[:, pl.ds(edge, 8), :], block)
    lanes = pl.ds(pl.multiple_of(place[0] * LANES, LANES), LANES)
    start(measured.at[0, :, :, lanes], whole.at[pl.ds(0, angles)])
    start(frac.at[0, :, lanes], whole.at[angles])
    for k in range(cols):
        whole[angles + 1, k : k + 1, :] = jnp.full((1, LANES), shift[0, k], jnp.int32).astype(F32)
    sent = []
    for k in range(slabs):
        copies[k].wait()
        sent.append(pltpu.make_async_copy(half.at[k], parts.at[k], done.at[k]))
        sent[k].start()
    for copy in copies[slabs:]:
        copy.wait()
    same[0 : angles + 2] = whole[:, pl.ds(pl.multiple_of(HALO * (1 - phase), HALO), HALO), :]
    rim = jnp.where(phase == 0, block[:, 7, :], block[:, 0, :])
    for k in range(same.shape[0] - angles - 2):
        lanes = slice(k // 2 * LANES, (k // 2 + 1) * LANES)
        same[angles + 2 + k] = rim[k % 2 * HALO : (k % 2 + 1) * HALO, lanes]
    cross[...] = whole[:, columns, :]
    for copy in sent:
        copy.wait()


def pack(place, index, other, same, table, volume, first, second, third, fourth, block, low, high, sem):
    depth, cols, _ = volume.shape
    angles = index.shape[1]
    start = pl.multiple_of(HALO - 8 * place[1], 8)
    copy = pltpu.make_async_copy(volume.at[:, pl.ds(start, 8), :], block, sem.at[0])
    copy.start()
    numbers = jnp.concatenate([index[...], other[...]], axis=1)
    count = table.shape[1]
    picker = (lax.broadcasted_iota(jnp.int32, (count, 2 * angles), 0) == numbers).astype(F32)
    flipped = jnp.dot(table[...], picker, precision=HIGH, preferred_element_type=F32)
    row = lax.broadcasted_iota(jnp.int32, (depth, LANES), 0)
    lane = lax.broadcasted_iota(jnp.int32, (depth, LANES), 1)
    weights = outer(flipped, (lane == row + place[0] * depth).astype(F32))
    left = place[1] == 0
    copy.wait()
    inner = jnp.where(left, block[:, 0, :], block[:, 7, :])
    slabs = volume.shape[2] // LANES
    for k in range(slabs):
        lanes = slice(k * LANES, (k + 1) * LANES)
        row = angles + 2 + 2 * k
        beside = jnp.concatenate([same[row], same[row + 1]], axis=0)
        low[:, lanes] = jnp.where(left, beside, inner[:, lanes])
        high[:, lanes] = jnp.where(left, inner[:, lanes], beside)
    for k, out in enumerate((first, second, third, fourth)):
        to = place[0] + k
        to = jnp.where(to >= slabs, to - slabs, to)
        lanes = pl.ds(pl.multiple_of(to * LANES, LANES), LANES)
        out[0] = weights[0:angles]
        out[1] = weights[angles:]
        out[2] = low[:, lanes]
        out[3] = high[:, lanes]


def arrange(place, own, other, same, cross, seen, share, steps):
    phase = place[1]
    angles = own.shape[0] - 2
    middle = pl.multiple_of(HALO * (1 - phase), HALO)
    side = pl.multiple_of(2 * HALO * phase, HALO)
    for to, inside, beyond in ((phase, own, same), (1 - phase, other, cross)):
        for ref, start in ((inside, middle), (beyond, side)):
            size = ref.shape[1]
            seen[to, pl.ds(start, size)] = jnp.swapaxes(ref[0:angles], 0, 1)
            share[to, pl.ds(start, size), :] = ref[angles]
            steps[to, pl.ds(start, size), :] = ref[angles + 1]


def core(
    place, steps, parts, a, b, c, d, seen, share, grad, weights, own, other,
    ext, field, canvas, beside,
):
    slabs, depth, half, width = parts.shape
    angles = seen.shape[2]
    phase = place[1]
    mine, theirs = ((a[k] + b[k]) + (c[k] + d[k]) for k in range(2))
    table = jnp.concatenate(
        [jnp.where(phase == 0, mine, theirs), jnp.where(phase == 0, theirs, mine)], axis=0
    )
    weights[...] = table
    for k, ref in enumerate((a, b, c, d)):
        source = place[0] - k
        source = jnp.where(source < 0, source + slabs, source)
        rows = pl.ds(pl.multiple_of(source * depth, depth), depth)
        beside[0, rows, :] = ref[2]
        beside[1, rows, :] = ref[3]
    nothing = jnp.zeros((2 * angles, width), F32)

    def put(columns, at):
        value = jnp.concatenate(columns, axis=1)
        value = jnp.dot(table, value, precision=HIGH, preferred_element_type=F32)
        for k in range(len(columns)):
            ext[at[k]] = value[:, k * width : (k + 1) * width]

    for base in range(0, half, 8):
        turned = [jnp.swapaxes(parts[s, :, base : base + 8, :], 0, 1) for s in range(slabs)]
        for k in range(0, 8, 2):
            columns = [
                jnp.concatenate([turned[s][k + i] for s in range(slabs)], axis=0)
                for i in range(2)
            ]
            put(columns, (base + k + 2, base + k + 3))
    put([beside[0], beside[1]], (1, half + 2))
    ext[0] = nothing
    ext[half + 3] = nothing
    grad[...] = jnp.zeros_like(grad)
    field[...] = jnp.zeros_like(field)
    outermost = jnp.where((phase == 0) & (place[2] == 0), 1, 2)
    for q in range(2):
        rows = slice(q * angles, (q + 1) * angles)
        for j in range(seen.shape[1]):
            at = j + steps[q, j] - 14

            @pl.when((at >= 1) & (at <= half + 1))
            def _(q=q, j=j, at=at, rows=rows):
                lower, upper = ext[at, rows, :], ext[at + 1, rows, :]
                part = share[q, j : j + 1, :]
                rest = 1.0 - part
                resid = (rest * lower + part * upper) - seen[q, j]
                value = jnp.sum(resid * (upper - lower), axis=0, keepdims=True)
                field[q, j : j + 1, :] = jnp.where(at >= outermost, value, 0.0)
                grad[at, rows, :] = grad[at, rows, :] + rest * resid
                grad[at + 1, rows, :] = grad[at + 1, rows, :] + part * resid

    canvas[...] = jnp.zeros_like(canvas)
    start = pl.multiple_of(HALO * phase, HALO)
    for q in range(2):
        canvas[q, pl.ds(start, seen.shape[1]), :] = field[q]
    own[...] = canvas[phase]
    other[...] = canvas[1 - phase]


def spread(grad, weights, out, staged, sems):
    slabs, half, depth, width = staged.shape
    table = weights[...].T
    copies = []
    for k in range(0, half, 2):
        pair = jnp.concatenate([grad[k + 2], grad[k + 3]], axis=1)
        value = jnp.dot(table, pair, precision=HIGH, preferred_element_type=F32)
        for chunk in range(slabs):
            part = value[chunk * depth : (chunk + 1) * depth]
            staged[chunk, k] = part[:, :width]
            staged[chunk, k + 1] = part[:, width:]
        if k % 4 == 2:
            columns = pl.ds(k - 2, 4)
            for to in range(2):
                target = out.at[pl.ds(to * slabs, slabs), columns]
                copies.append(
                    pltpu.make_async_copy(staged.at[:, columns], target, sems.at[len(copies)])
                )
                copies[-1].start()
    for copy in copies:
        copy.wait()


def merge(place, own, other, kept, side_o, side_e):
    total = own[...] + other[...]
    kept[...] = total[EDGE : EDGE + SPAN]
    left, right = total[0:ROWS], total[total.shape[0] - ROWS :]
    odd = place[3] == 1
    side_o[...] = jnp.where(odd, right, left)
    side_e[...] = jnp.where(odd, left, right)


def collect(place, kept, side_o, side_e, out):
    odd = place[3] == 1
    from_left = jnp.where(odd, side_e[...], side_o[...])
    from_right = jnp.where(odd, side_o[...], side_e[...])
    out[0:ROWS, :] = kept[0:ROWS] + from_left
    out[ROWS:, :] = kept[ROWS:] + from_right


def diffuse(last, place, a, b, c, d, field, chunks):
    cols = field.shape[1]
    for k, ref in enumerate((a, b, c, d)):
        source = place[0] - k
        chunks[jnp.where(source < 0, source + 4, source)] = ref[...]
    wide = jnp.concatenate([chunks[k] for k in range(chunks.shape[0])], axis=1)
    height, total = wide.shape
    row = lax.broadcasted_iota(jnp.int32, wide.shape, 0)
    lane = lax.broadcasted_iota(jnp.int32, wide.shape, 1)
    outside = ((row < EDGE) & (place[2] == 0)) | ((row >= EDGE + cols) & (place[2] == last))
    for _ in range(ITS):
        after = pltpu.roll(wide, height - 1, 0)
        before = pltpu.roll(wide, 1, 0)
        right = jnp.where(lane == total - 1, 0.0, pltpu.roll(wide, total - 1, 1))
        left = jnp.where(lane == 0, 0.0, pltpu.roll(wide, 1, 1))
        laplace = after + before + right + left - 4.0 * wide
        wide = jnp.where(outside, 0.0, wide + DIFFUSION * laplace)
    field[0] = wide[EDGE : EDGE + cols]


def finish(parts, image, block, sems):
    slabs = parts.shape[0] // 2
    copies = []
    for k in range(image.shape[1] // 8):
        phase, start = divmod(8 * k, HALO)
        for chunk in range(slabs):
            block[k, :, :, chunk * LANES : (chunk + 1) * LANES] = jnp.swapaxes(
                parts[phase * slabs + chunk, start : start + 8], 0, 1
            )
        columns = pl.ds(8 * k, 8)
        copies.append(pltpu.make_async_copy(block.at[k], image.at[:, columns, :], sems.at[k]))
        copies[k].start()
    for copy in copies:
        copy.wait()


def move(block, target):
    phases, tiles = lax.axis_size("phase"), lax.axis_size("tile")
    route = []
    for phase in range(phases):
        for tile in range(tiles):
            to_phase, to_tile = target(phase, tile)
            if 0 <= to_tile < tiles:
                route.append((phase * tiles + tile, to_phase * tiles + to_tile))
    return lax.ppermute(block, ("phase", "tile"), route)


def body(volume, frac, shift, angle_index, depth_weights, measured):
    depth, cols, height = volume.shape
    angles = angle_index.shape[1]
    slabs, tiles, phases = (lax.axis_size(a) for a in ("slab", "tile", "phase"))
    group = phases * slabs
    tile = lax.axis_index("tile")
    place = jnp.stack(
        [lax.axis_index("slab"), lax.axis_index("phase"), tile, tile % 2]
    ).astype(jnp.int32)
    octet = pltpu.VMEM((depth, 8, height), F32)
    blocks = pltpu.VMEM((cols // 8, depth, 8, height), F32)
    dma = pltpu.SemaphoreType.DMA

    def toward(phase, tile):
        return phase, tile + 1 - 2 * phase

    def across(phase, tile):
        return 1 - phase, tile - 1 + 2 * phase

    def partner(phase, tile):
        return 1 - phase, tile

    def around(block, distance):
        return lax.ppermute(block, "slab", [(i, (i + distance) % slabs) for i in range(slabs)])

    rim = depth * height // (HALO * LANES)
    bundles = [(angles + 2 + more, size, LANES) for more, size in ((0, cols), (rim, HALO), (0, HALO))]
    message = (slabs, depth, HALO, LANES)
    bundle_own, same, cross, parts = call(
        load,
        bundles + [message],
        [SMEM] * 2 + [ANY] * 3,
        [octet, pltpu.VMEM(message, F32), dma((slabs + 3,)), dma((slabs,))],
        [VMEM] * 3 + [ANY],
        limit=ROOM,
    )(place, shift, measured, frac, volume)
    index_other = move(angle_index, partner)
    bundle_other = move(bundle_own, partner)
    parts, index_other = lax.optimization_barrier((parts, index_other))
    parts = lax.all_to_all(parts, "slab", 0, 0, tiled=True)
    same = move(same, toward)
    cross = move(cross, across)
    wide = pltpu.VMEM((depth, height), F32)
    extras = call(
        pack,
        [(4, depth, LANES)] * slabs,
        [SMEM] + [VMEM] * 4 + [ANY],
        [octet, wide, wide, dma((1,))],
    )(place, angle_index, index_other, same, depth_weights.T, volume)
    extras = [extras[0]] + [around(extras[k], k) for k in range(1, slabs)]
    seen, share, steps = call(
        arrange,
        [(phases, SPAN, angles, LANES), (phases, SPAN, LANES), (phases, SPAN, LANES)],
        [SMEM] + [VMEM] * 4,
    )(place, bundle_own, bundle_other, same, cross)
    steps = steps[:, :, 0].astype(jnp.int32)
    parts, seen, share, steps, *extras = lax.optimization_barrier(
        (parts, seen, share, steps, *extras)
    )
    window, side, canvas = (SPAN, LANES), (ROWS, LANES), (4 * HALO, LANES)
    stack = (HALO + 4, 2 * angles, LANES)
    grad, weights, own, other = call(
        core,
        [stack, (2 * angles, LANES), canvas, canvas],
        [SMEM] * 2 + [VMEM] * 7,
        [
            pltpu.VMEM(stack, F32),
            pltpu.VMEM((phases, SPAN, LANES), F32),
            pltpu.VMEM((phases,) + canvas, F32),
            pltpu.VMEM((2, slabs * depth, LANES), F32),
        ],
    )(place, steps, parts, *extras, seen, share)
    (parts,) = call(
        spread,
        [(group, HALO, depth, LANES)],
        [VMEM] * 2,
        [pltpu.VMEM((slabs, HALO, depth, LANES), F32), dma((HALO // 2,))],
        [ANY],
        limit=50,
    )(grad, weights)
    other = move(other, partner)
    parts, other = lax.optimization_barrier((parts, other))
    parts = lax.all_to_all(parts, ("phase", "slab"), 0, 0, tiled=True)
    kept, side_o, side_e = call(merge, [window, side, side], [SMEM] + [VMEM] * 2)(
        place, own, other
    )
    pairs_e = [(i, i ^ 1) for i in range(tiles)]
    pairs_o = [(i, ((i + 1) ^ 1) - 1) for i in range(1, tiles - 1)]
    (field,) = call(collect, [window], [SMEM] + [VMEM] * 3)(
        place, kept, lax.ppermute(side_o, "tile", pairs_o), lax.ppermute(side_e, "tile", pairs_e)
    )
    fields = [field] + [around(field, k) for k in range(1, slabs)]

    def ending(*refs):
        diffuse(tiles - 1, *refs)

    (image,) = call(
        finish, [(depth, cols, height)], [VMEM], [blocks, dma((cols // 8,))], [ANY]
    )(parts)
    image, *fields = lax.optimization_barrier((image, *fields))
    (field,) = call(
        ending,
        [(1, cols, height)],
        [SMEM] + [VMEM] * 4,
        [pltpu.VMEM((slabs,) + window, F32)],
    )(place, *fields)
    return image, field


def solution(mesh):
    return jax.shard_map(
        body,
        mesh=mesh,
        in_specs=(
            P("slab", "tile", None),
            P("phase", "tile", None),
            P("phase", "tile"),
            P("phase", None),
            P(None, "slab"),
            P("phase", None, "tile", None),
        ),
        out_specs=(P("slab", "tile", None), P("phase", "tile", None)),
        check_vma=False,
    )
```

```python
import jax
import jax.numpy as jnp
from jax import lax
from jax.experimental import pallas as pl
from jax.experimental.pallas import tpu as pltpu
from jax.sharding import PartitionSpec as P

HALO = 16
ITS = 4
DIFFUSION = 0.2
EDGE = 8
SPAN = 3 * HALO
ROWS = 24
LANES = 128
ROOM = 56
HIGH = lax.Precision.HIGHEST
F32 = jnp.float32
VMEM = pl.BlockSpec(memory_space=pltpu.VMEM)
SMEM = pl.BlockSpec(memory_space=pltpu.SMEM)
ANY = pl.BlockSpec(memory_space=pltpu.HBM)


def call(kernel, outs, in_specs, scratch=(), out_specs=None, aliases=None, limit=16):
    return pl.pallas_call(
        kernel,
        out_shape=[jax.ShapeDtypeStruct(o, F32) for o in outs],
        in_specs=in_specs,
        out_specs=out_specs or [VMEM] * len(outs),
        scratch_shapes=list(scratch),
        input_output_aliases=aliases or {},
        compiler_params=pltpu.CompilerParams(vmem_limit_bytes=limit << 20),
        cost_estimate=pl.CostEstimate(flops=1 << 22, bytes_accessed=1 << 21, transcendentals=0),
    )


def outer(a, b):
    return lax.dot_general(
        a, b, (((0,), (0,)), ((), ())), precision=HIGH, preferred_element_type=F32
    )


def load(
    place, shift, measured, frac, volume, whole, same, cross, first, second, third, fourth,
    block, sems,
):
    angles, cols = measured.shape[1:3]
    phase = place[1]
    copies = []

    def start(source, target):
        copies.append(pltpu.make_async_copy(source, target, sems.at[len(copies)]))
        copies[-1].start()

    columns = pl.ds(pl.multiple_of(HALO * phase, HALO), HALO)
    shares = (first, second, third, fourth)
    for k, share in enumerate(shares):
        to = place[0] + k
        to = jnp.where(to >= len(shares), to - len(shares), to)
        part = pl.ds(pl.multiple_of(to * LANES, LANES), LANES)
        start(volume.at[:, columns, part], share)
    edge = pl.multiple_of((cols - 8) * (1 - phase), 8)
    start(volume.at[:, pl.ds(edge, 8), :], block)
    lanes = pl.ds(pl.multiple_of(place[0] * LANES, LANES), LANES)
    start(measured.at[0, :, :, lanes], whole.at[pl.ds(0, angles)])
    start(frac.at[0, :, lanes], whole.at[angles])
    for k in range(cols):
        whole[angles + 1, k : k + 1, :] = jnp.full((1, LANES), shift[0, k], jnp.int32).astype(F32)
    for copy in copies:
        copy.wait()
    same[0 : angles + 2] = whole[:, pl.ds(pl.multiple_of(HALO * (1 - phase), HALO), HALO), :]
    rim = jnp.where(phase == 0, block[:, 7, :], block[:, 0, :])
    for k in range(same.shape[0] - angles - 2):
        lanes = slice(k // 2 * LANES, (k // 2 + 1) * LANES)
        same[angles + 2 + k] = rim[k % 2 * HALO : (k % 2 + 1) * HALO, lanes]
    cross[...] = whole[:, columns, :]


def pack(place, index, other, same, table, volume, first, second, third, fourth, block, low, high, sem):
    depth, cols, _ = volume.shape
    angles = index.shape[1]
    start = pl.multiple_of(HALO - 8 * place[1], 8)
    copy = pltpu.make_async_copy(volume.at[:, pl.ds(start, 8), :], block, sem.at[0])
    copy.start()
    numbers = jnp.concatenate([index[...], other[...]], axis=1)
    count = table.shape[1]
    picker = (lax.broadcasted_iota(jnp.int32, (count, 2 * angles), 0) == numbers).astype(F32)
    flipped = jnp.dot(table[...], picker, precision=HIGH, preferred_element_type=F32)
    row = lax.broadcasted_iota(jnp.int32, (depth, LANES), 0)
    lane = lax.broadcasted_iota(jnp.int32, (depth, LANES), 1)
    weights = outer(flipped, (lane == row + place[0] * depth).astype(F32))
    left = place[1] == 0
    copy.wait()
    inner = jnp.where(left, block[:, 0, :], block[:, 7, :])
    slabs = volume.shape[2] // LANES
    for k in range(slabs):
        lanes = slice(k * LANES, (k + 1) * LANES)
        row = angles + 2 + 2 * k
        beside = jnp.concatenate([same[row], same[row + 1]], axis=0)
        low[:, lanes] = jnp.where(left, beside, inner[:, lanes])
        high[:, lanes] = jnp.where(left, inner[:, lanes], beside)
    for k, out in enumerate((first, second, third, fourth)):
        to = place[0] + k
        to = jnp.where(to >= slabs, to - slabs, to)
        lanes = pl.ds(pl.multiple_of(to * LANES, LANES), LANES)
        out[0] = weights[0:angles]
        out[1] = weights[angles:]
        out[2] = low[:, lanes]
        out[3] = high[:, lanes]


def arrange(place, own, other, same, cross, seen, share, steps):
    phase = place[1]
    angles = own.shape[0] - 2
    middle = pl.multiple_of(HALO * (1 - phase), HALO)
    side = pl.multiple_of(2 * HALO * phase, HALO)
    for to, inside, beyond in ((phase, own, same), (1 - phase, other, cross)):
        for ref, start in ((inside, middle), (beyond, side)):
            size = ref.shape[1]
            seen[to, pl.ds(start, size)] = jnp.swapaxes(ref[0:angles], 0, 1)
            share[to, pl.ds(start, size), :] = ref[angles]
            steps[to, pl.ds(start, size), :] = ref[angles + 1]


def core(
    place, steps, first, second, third, fourth, a, b, c, d, seen, share, grad, weights, own, other,
    ext, field, canvas, beside, parts,
):
    slabs, depth, half, width = parts.shape
    angles = seen.shape[2]
    phase = place[1]
    mine, theirs = ((a[k] + b[k]) + (c[k] + d[k]) for k in range(2))
    table = jnp.concatenate(
        [jnp.where(phase == 0, mine, theirs), jnp.where(phase == 0, theirs, mine)], axis=0
    )
    weights[...] = table
    for k, ref in enumerate((a, b, c, d)):
        source = place[0] - k
        source = jnp.where(source < 0, source + slabs, source)
        rows = pl.ds(pl.multiple_of(source * depth, depth), depth)
        beside[0, rows, :] = ref[2]
        beside[1, rows, :] = ref[3]
        parts[source] = (first, second, third, fourth)[k][...]
    nothing = jnp.zeros((2 * angles, width), F32)

    def put(columns, at):
        value = jnp.concatenate(columns, axis=1)
        value = jnp.dot(table, value, precision=HIGH, preferred_element_type=F32)
        for k in range(len(columns)):
            ext[at[k]] = value[:, k * width : (k + 1) * width]

    for base in range(0, half, 8):
        turned = [jnp.swapaxes(parts[s, :, base : base + 8, :], 0, 1) for s in range(slabs)]
        for k in range(0, 8, 2):
            columns = [
                jnp.concatenate([turned[s][k + i] for s in range(slabs)], axis=0)
                for i in range(2)
            ]
            put(columns, (base + k + 2, base + k + 3))
    put([beside[0], beside[1]], (1, half + 2))
    ext[0] = nothing
    ext[half + 3] = nothing
    grad[...] = jnp.zeros_like(grad)
    field[...] = jnp.zeros_like(field)
    outermost = jnp.where((phase == 0) & (place[2] == 0), 1, 2)
    for q in range(2):
        rows = slice(q * angles, (q + 1) * angles)
        for j in range(seen.shape[1]):
            at = j + steps[q, j] - 14

            @pl.when((at >= 1) & (at <= half + 1))
            def _(q=q, j=j, at=at, rows=rows):
                lower, upper = ext[at, rows, :], ext[at + 1, rows, :]
                part = share[q, j : j + 1, :]
                rest = 1.0 - part
                resid = (rest * lower + part * upper) - seen[q, j]
                value = jnp.sum(resid * (upper - lower), axis=0, keepdims=True)
                field[q, j : j + 1, :] = jnp.where(at >= outermost, value, 0.0)
                grad[at, rows, :] = grad[at, rows, :] + rest * resid
                grad[at + 1, rows, :] = grad[at + 1, rows, :] + part * resid

    canvas[...] = jnp.zeros_like(canvas)
    start = pl.multiple_of(HALO * phase, HALO)
    for q in range(2):
        canvas[q, pl.ds(start, seen.shape[1]), :] = field[q]
    own[...] = canvas[phase]
    other[...] = canvas[1 - phase]


def spread(grad, weights, out, staged, sems):
    slabs, half, depth, width = staged.shape
    table = weights[...].T
    copies = []
    for k in range(0, half, 2):
        pair = jnp.concatenate([grad[k + 2], grad[k + 3]], axis=1)
        value = jnp.dot(table, pair, precision=HIGH, preferred_element_type=F32)
        for chunk in range(slabs):
            part = value[chunk * depth : (chunk + 1) * depth]
            staged[chunk, k] = part[:, :width]
            staged[chunk, k + 1] = part[:, width:]
        if k % 4 == 2:
            columns = pl.ds(k - 2, 4)
            for to in range(2):
                target = out.at[pl.ds(to * slabs, slabs), columns]
                copies.append(
                    pltpu.make_async_copy(staged.at[:, columns], target, sems.at[len(copies)])
                )
                copies[-1].start()
    for copy in copies:
        copy.wait()


def merge(place, own, other, kept, side_o, side_e):
    total = own[...] + other[...]
    kept[...] = total[EDGE : EDGE + SPAN]
    left, right = total[0:ROWS], total[total.shape[0] - ROWS :]
    odd = place[3] == 1
    side_o[...] = jnp.where(odd, right, left)
    side_e[...] = jnp.where(odd, left, right)


def collect(place, kept, side_o, side_e, out):
    odd = place[3] == 1
    from_left = jnp.where(odd, side_e[...], side_o[...])
    from_right = jnp.where(odd, side_o[...], side_e[...])
    out[0:ROWS, :] = kept[0:ROWS] + from_left
    out[ROWS:, :] = kept[ROWS:] + from_right


def diffuse(last, place, a, b, c, d, field, chunks):
    cols = field.shape[1]
    for k, ref in enumerate((a, b, c, d)):
        source = place[0] - k
        chunks[jnp.where(source < 0, source + 4, source)] = ref[...]
    wide = jnp.concatenate([chunks[k] for k in range(chunks.shape[0])], axis=1)
    height, total = wide.shape
    row = lax.broadcasted_iota(jnp.int32, wide.shape, 0)
    lane = lax.broadcasted_iota(jnp.int32, wide.shape, 1)
    outside = ((row < EDGE) & (place[2] == 0)) | ((row >= EDGE + cols) & (place[2] == last))
    for _ in range(ITS):
        after = pltpu.roll(wide, height - 1, 0)
        before = pltpu.roll(wide, 1, 0)
        right = jnp.where(lane == total - 1, 0.0, pltpu.roll(wide, total - 1, 1))
        left = jnp.where(lane == 0, 0.0, pltpu.roll(wide, 1, 1))
        laplace = after + before + right + left - 4.0 * wide
        wide = jnp.where(outside, 0.0, wide + DIFFUSION * laplace)
    field[0] = wide[EDGE : EDGE + cols]


def finish(parts, image, block, sems):
    slabs = parts.shape[0] // 2
    copies = []
    for k in range(image.shape[1] // 8):
        phase, start = divmod(8 * k, HALO)
        for chunk in range(slabs):
            block[k, :, :, chunk * LANES : (chunk + 1) * LANES] = jnp.swapaxes(
                parts[phase * slabs + chunk, start : start + 8], 0, 1
            )
        columns = pl.ds(8 * k, 8)
        copies.append(pltpu.make_async_copy(block.at[k], image.at[:, columns, :], sems.at[k]))
        copies[k].start()
    for copy in copies:
        copy.wait()


def move(block, target):
    phases, tiles = lax.axis_size("phase"), lax.axis_size("tile")
    route = []
    for phase in range(phases):
        for tile in range(tiles):
            to_phase, to_tile = target(phase, tile)
            if 0 <= to_tile < tiles:
                route.append((phase * tiles + tile, to_phase * tiles + to_tile))
    return lax.ppermute(block, ("phase", "tile"), route)


def body(volume, frac, shift, angle_index, depth_weights, measured):
    depth, cols, height = volume.shape
    angles = angle_index.shape[1]
    slabs, tiles, phases = (lax.axis_size(a) for a in ("slab", "tile", "phase"))
    group = phases * slabs
    tile = lax.axis_index("tile")
    place = jnp.stack(
        [lax.axis_index("slab"), lax.axis_index("phase"), tile, tile % 2]
    ).astype(jnp.int32)
    octet = pltpu.VMEM((depth, 8, height), F32)
    blocks = pltpu.VMEM((cols // 8, depth, 8, height), F32)
    dma = pltpu.SemaphoreType.DMA

    def toward(phase, tile):
        return phase, tile + 1 - 2 * phase

    def across(phase, tile):
        return 1 - phase, tile - 1 + 2 * phase

    def partner(phase, tile):
        return 1 - phase, tile

    def around(block, distance):
        return lax.ppermute(block, "slab", [(i, (i + distance) % slabs) for i in range(slabs)])

    rim = depth * height // (HALO * LANES)
    bundles = [(angles + 2 + more, size, LANES) for more, size in ((0, cols), (rim, HALO), (0, HALO))]
    message = (slabs, depth, HALO, LANES)
    bundle_own, same, cross, *parts = call(
        load,
        bundles + [message[1:]] * slabs,
        [SMEM] * 2 + [ANY] * 3,
        [octet, dma((slabs + 3,))],
        limit=ROOM,
    )(place, shift, measured, frac, volume)
    index_other = move(angle_index, partner)
    bundle_own, same, cross, index_other, *parts = lax.optimization_barrier(
        (bundle_own, same, cross, index_other, *parts)
    )
    bundle_other = move(bundle_own, partner)
    parts = [parts[0]] + [around(parts[k], k) for k in range(1, slabs)]
    same = move(same, toward)
    cross = move(cross, across)
    wide = pltpu.VMEM((depth, height), F32)
    extras = call(
        pack,
        [(4, depth, LANES)] * slabs,
        [SMEM] + [VMEM] * 4 + [ANY],
        [octet, wide, wide, dma((1,))],
    )(place, angle_index, index_other, same, depth_weights.T, volume)
    extras = [extras[0]] + [around(extras[k], k) for k in range(1, slabs)]
    seen, share, steps = call(
        arrange,
        [(phases, SPAN, angles, LANES), (phases, SPAN, LANES), (phases, SPAN, LANES)],
        [SMEM] + [VMEM] * 4,
    )(place, bundle_own, bundle_other, same, cross)
    steps = steps[:, :, 0].astype(jnp.int32)
    window, side, canvas = (SPAN, LANES), (ROWS, LANES), (4 * HALO, LANES)
    stack = (HALO + 4, 2 * angles, LANES)
    grad, weights, own, other = call(
        core,
        [stack, (2 * angles, LANES), canvas, canvas],
        [SMEM] * 2 + [VMEM] * 10,
        [
            pltpu.VMEM(stack, F32),
            pltpu.VMEM((phases, SPAN, LANES), F32),
            pltpu.VMEM((phases,) + canvas, F32),
            pltpu.VMEM((2, slabs * depth, LANES), F32),
            pltpu.VMEM(message, F32),
        ],
    )(place, steps, *parts, *extras, seen, share)
    (parts,) = call(
        spread,
        [(group, HALO, depth, LANES)],
        [VMEM] * 2,
        [pltpu.VMEM((slabs, HALO, depth, LANES), F32), dma((HALO // 2,))],
        [ANY],
        limit=50,
    )(grad, weights)
    other = move(other, partner)
    parts, other = lax.optimization_barrier((parts, other))
    parts = lax.all_to_all(parts, ("phase", "slab"), 0, 0, tiled=True)
    kept, side_o, side_e = call(merge, [window, side, side], [SMEM] + [VMEM] * 2)(
        place, own, other
    )
    pairs_e = [(i, i ^ 1) for i in range(tiles)]
    pairs_o = [(i, ((i + 1) ^ 1) - 1) for i in range(1, tiles - 1)]
    (field,) = call(collect, [window], [SMEM] + [VMEM] * 3)(
        place, kept, lax.ppermute(side_o, "tile", pairs_o), lax.ppermute(side_e, "tile", pairs_e)
    )
    fields = [field] + [around(field, k) for k in range(1, slabs)]

    def ending(*refs):
        diffuse(tiles - 1, *refs)

    (image,) = call(
        finish, [(depth, cols, height)], [VMEM], [blocks, dma((cols // 8,))], [ANY]
    )(parts)
    image, *fields = lax.optimization_barrier((image, *fields))
    (field,) = call(
        ending,
        [(1, cols, height)],
        [SMEM] + [VMEM] * 4,
        [pltpu.VMEM((slabs,) + window, F32)],
    )(place, *fields)
    return image, field


def solution(mesh):
    return jax.shard_map(
        body,
        mesh=mesh,
        in_specs=(
            P("slab", "tile", None),
            P("phase", "tile", None),
            P("phase", "tile"),
            P("phase", None),
            P(None, "slab"),
            P("phase", None, "tile", None),
        ),
        out_specs=(P("slab", "tile", None), P("phase", "tile", None)),
        check_vma=False,
    )
```

```python
import jax
import jax.numpy as jnp
from jax import lax
from jax.experimental import pallas as pl
from jax.experimental.pallas import tpu as pltpu
from jax.sharding import PartitionSpec as P

HALO = 16
ITS = 4
DIFFUSION = 0.2
EDGE = 8
SPAN = 3 * HALO
ROWS = 24
LANES = 128
ROOM = 56
HIGH = lax.Precision.HIGHEST
F32 = jnp.float32
VMEM = pl.BlockSpec(memory_space=pltpu.VMEM)
SMEM = pl.BlockSpec(memory_space=pltpu.SMEM)
ANY = pl.BlockSpec(memory_space=pltpu.HBM)


def call(kernel, outs, in_specs, scratch=(), out_specs=None, aliases=None, limit=16):
    return pl.pallas_call(
        kernel,
        out_shape=[jax.ShapeDtypeStruct(o, F32) for o in outs],
        in_specs=in_specs,
        out_specs=out_specs or [VMEM] * len(outs),
        scratch_shapes=list(scratch),
        input_output_aliases=aliases or {},
        compiler_params=pltpu.CompilerParams(vmem_limit_bytes=limit << 20),
        cost_estimate=pl.CostEstimate(flops=1 << 22, bytes_accessed=1 << 21, transcendentals=0),
    )


def outer(a, b):
    return lax.dot_general(
        a, b, (((0,), (0,)), ((), ())), precision=HIGH, preferred_element_type=F32
    )


def load(
    place, shift, measured, frac, volume, whole, same, cross, first, second, third, fourth,
    block, sems,
):
    angles, cols = measured.shape[1:3]
    phase = place[1]
    copies = []

    def start(source, target):
        copies.append(pltpu.make_async_copy(source, target, sems.at[len(copies)]))
        copies[-1].start()

    columns = pl.ds(pl.multiple_of(HALO * phase, HALO), HALO)
    shares = (first, second, third, fourth)
    for k, share in enumerate(shares):
        to = place[0] + k
        to = jnp.where(to >= len(shares), to - len(shares), to)
        part = pl.ds(pl.multiple_of(to * LANES, LANES), LANES)
        start(volume.at[:, columns, part], share)
    edge = pl.multiple_of((cols - 8) * (1 - phase), 8)
    start(volume.at[:, pl.ds(edge, 8), :], block)
    lanes = pl.ds(pl.multiple_of(place[0] * LANES, LANES), LANES)
    start(measured.at[0, :, :, lanes], whole.at[pl.ds(0, angles)])
    start(frac.at[0, :, lanes], whole.at[angles])
    for k in range(cols):
        whole[angles + 1, k : k + 1, :] = jnp.full((1, LANES), shift[0, k], jnp.int32).astype(F32)
    for copy in copies:
        copy.wait()
    same[0 : angles + 2] = whole[:, pl.ds(pl.multiple_of(HALO * (1 - phase), HALO), HALO), :]
    rim = jnp.where(phase == 0, block[:, 7, :], block[:, 0, :])
    for k in range(same.shape[0] - angles - 2):
        lanes = slice(k // 2 * LANES, (k // 2 + 1) * LANES)
        same[angles + 2 + k] = rim[k % 2 * HALO : (k % 2 + 1) * HALO, lanes]
    cross[...] = whole[:, columns, :]


def pack(place, index, other, same, table, volume, first, second, third, fourth, block, low, high, sem):
    depth, cols, _ = volume.shape
    angles = index.shape[1]
    start = pl.multiple_of(HALO - 8 * place[1], 8)
    copy = pltpu.make_async_copy(volume.at[:, pl.ds(start, 8), :], block, sem.at[0])
    copy.start()
    numbers = jnp.concatenate([index[...], other[...]], axis=1)
    count = table.shape[1]
    picker = (lax.broadcasted_iota(jnp.int32, (count, 2 * angles), 0) == numbers).astype(F32)
    flipped = jnp.dot(table[...], picker, precision=HIGH, preferred_element_type=F32)
    row = lax.broadcasted_iota(jnp.int32, (depth, LANES), 0)
    lane = lax.broadcasted_iota(jnp.int32, (depth, LANES), 1)
    weights = outer(flipped, (lane == row + place[0] * depth).astype(F32))
    left = place[1] == 0
    copy.wait()
    inner = jnp.where(left, block[:, 0, :], block[:, 7, :])
    slabs = volume.shape[2] // LANES
    for k in range(slabs):
        lanes = slice(k * LANES, (k + 1) * LANES)
        row = angles + 2 + 2 * k
        beside = jnp.concatenate([same[row], same[row + 1]], axis=0)
        low[:, lanes] = jnp.where(left, beside, inner[:, lanes])
        high[:, lanes] = jnp.where(left, inner[:, lanes], beside)
    for k, out in enumerate((first, second, third, fourth)):
        to = place[0] + k
        to = jnp.where(to >= slabs, to - slabs, to)
        lanes = pl.ds(pl.multiple_of(to * LANES, LANES), LANES)
        out[0] = weights[0:angles]
        out[1] = weights[angles:]
        out[2] = low[:, lanes]
        out[3] = high[:, lanes]


def arrange(place, own, other, same, cross, seen, share, steps):
    phase = place[1]
    angles = own.shape[0] - 2
    middle = pl.multiple_of(HALO * (1 - phase), HALO)
    side = pl.multiple_of(2 * HALO * phase, HALO)
    for to, inside, beyond in ((phase, own, same), (1 - phase, other, cross)):
        for ref, start in ((inside, middle), (beyond, side)):
            size = ref.shape[1]
            seen[to, pl.ds(start, size)] = jnp.swapaxes(ref[0:angles], 0, 1)
            share[to, pl.ds(start, size), :] = ref[angles]
            steps[to, pl.ds(start, size), :] = ref[angles + 1]


def core(
    place, steps, first, second, third, fourth, a, b, c, d, seen, share, grad, weights, own, other,
    ext, field, canvas, beside, parts,
):
    slabs, depth, half, width = parts.shape
    angles = seen.shape[2]
    phase = place[1]
    mine, theirs = ((a[k] + b[k]) + (c[k] + d[k]) for k in range(2))
    table = jnp.concatenate(
        [jnp.where(phase == 0, mine, theirs), jnp.where(phase == 0, theirs, mine)], axis=0
    )
    weights[...] = table
    for k, ref in enumerate((a, b, c, d)):
        source = place[0] - k
        source = jnp.where(source < 0, source + slabs, source)
        rows = pl.ds(pl.multiple_of(source * depth, depth), depth)
        beside[0, rows, :] = ref[2]
        beside[1, rows, :] = ref[3]
        parts[source] = (first, second, third, fourth)[k][...]
    nothing = jnp.zeros((2 * angles, width), F32)

    def put(columns, at):
        value = jnp.concatenate(columns, axis=1)
        value = jnp.dot(table, value, precision=HIGH, preferred_element_type=F32)
        for k in range(len(columns)):
            ext[at[k]] = value[:, k * width : (k + 1) * width]

    for base in range(0, half, 8):
        turned = [jnp.swapaxes(parts[s, :, base : base + 8, :], 0, 1) for s in range(slabs)]
        for k in range(0, 8, 2):
            columns = [
                jnp.concatenate([turned[s][k + i] for s in range(slabs)], axis=0)
                for i in range(2)
            ]
            put(columns, (base + k + 2, base + k + 3))
    put([beside[0], beside[1]], (1, half + 2))
    ext[0] = nothing
    ext[half + 3] = nothing
    grad[...] = jnp.zeros_like(grad)
    field[...] = jnp.zeros_like(field)
    outermost = jnp.where((phase == 0) & (place[2] == 0), 1, 2)
    for q in range(2):
        rows = slice(q * angles, (q + 1) * angles)
        for j in range(seen.shape[1]):
            at = j + steps[q, j] - 14

            @pl.when((at >= 1) & (at <= half + 1))
            def _(q=q, j=j, at=at, rows=rows):
                lower, upper = ext[at, rows, :], ext[at + 1, rows, :]
                part = share[q, j : j + 1, :]
                rest = 1.0 - part
                resid = (rest * lower + part * upper) - seen[q, j]
                value = jnp.sum(resid * (upper - lower), axis=0, keepdims=True)
                field[q, j : j + 1, :] = jnp.where(at >= outermost, value, 0.0)
                grad[at, rows, :] = grad[at, rows, :] + rest * resid
                grad[at + 1, rows, :] = grad[at + 1, rows, :] + part * resid

    canvas[...] = jnp.zeros_like(canvas)
    start = pl.multiple_of(HALO * phase, HALO)
    for q in range(2):
        canvas[q, pl.ds(start, seen.shape[1]), :] = field[q]
    own[...] = canvas[phase]
    other[...] = canvas[1 - phase]


def spread(grad, weights, out, staged, sems):
    slabs, half, depth, width = staged.shape
    table = weights[...].T
    copies = []
    for k in range(0, half, 2):
        pair = jnp.concatenate([grad[k + 2], grad[k + 3]], axis=1)
        value = jnp.dot(table, pair, precision=HIGH, preferred_element_type=F32)
        for chunk in range(slabs):
            part = value[chunk * depth : (chunk + 1) * depth]
            staged[chunk, k] = part[:, :width]
            staged[chunk, k + 1] = part[:, width:]
        if k % 4 == 2:
            columns = pl.ds(k - 2, 4)
            for to in range(2):
                target = out.at[pl.ds(to * slabs, slabs), columns]
                copies.append(
                    pltpu.make_async_copy(staged.at[:, columns], target, sems.at[len(copies)])
                )
                copies[-1].start()
    for copy in copies:
        copy.wait()


def merge(place, own, other, kept, side_o, side_e):
    total = own[...] + other[...]
    kept[...] = total[EDGE : EDGE + SPAN]
    left, right = total[0:ROWS], total[total.shape[0] - ROWS :]
    odd = place[3] == 1
    side_o[...] = jnp.where(odd, right, left)
    side_e[...] = jnp.where(odd, left, right)


def collect(place, kept, side_o, side_e, out):
    odd = place[3] == 1
    from_left = jnp.where(odd, side_e[...], side_o[...])
    from_right = jnp.where(odd, side_o[...], side_e[...])
    out[0:ROWS, :] = kept[0:ROWS] + from_left
    out[ROWS:, :] = kept[ROWS:] + from_right


def diffuse(last, place, a, b, c, d, field, chunks):
    cols = field.shape[1]
    for k, ref in enumerate((a, b, c, d)):
        source = place[0] - k
        chunks[jnp.where(source < 0, source + 4, source)] = ref[...]
    wide = jnp.concatenate([chunks[k] for k in range(chunks.shape[0])], axis=1)
    height, total = wide.shape
    row = lax.broadcasted_iota(jnp.int32, wide.shape, 0)
    lane = lax.broadcasted_iota(jnp.int32, wide.shape, 1)
    outside = ((row < EDGE) & (place[2] == 0)) | ((row >= EDGE + cols) & (place[2] == last))
    for _ in range(ITS):
        after = pltpu.roll(wide, height - 1, 0)
        before = pltpu.roll(wide, 1, 0)
        right = jnp.where(lane == total - 1, 0.0, pltpu.roll(wide, total - 1, 1))
        left = jnp.where(lane == 0, 0.0, pltpu.roll(wide, 1, 1))
        laplace = after + before + right + left - 4.0 * wide
        wide = jnp.where(outside, 0.0, wide + DIFFUSION * laplace)
    field[0] = wide[EDGE : EDGE + cols]


def finish(parts, image, block, sems):
    slabs = parts.shape[0] // 2
    copies = []
    for k in range(image.shape[1] // 8):
        phase, start = divmod(8 * k, HALO)
        for chunk in range(slabs):
            block[k, :, :, chunk * LANES : (chunk + 1) * LANES] = jnp.swapaxes(
                parts[phase * slabs + chunk, start : start + 8], 0, 1
            )
        columns = pl.ds(8 * k, 8)
        copies.append(pltpu.make_async_copy(block.at[k], image.at[:, columns, :], sems.at[k]))
        copies[k].start()
    for copy in copies:
        copy.wait()


def move(block, target):
    phases, tiles = lax.axis_size("phase"), lax.axis_size("tile")
    route = []
    for phase in range(phases):
        for tile in range(tiles):
            to_phase, to_tile = target(phase, tile)
            if 0 <= to_tile < tiles:
                route.append((phase * tiles + tile, to_phase * tiles + to_tile))
    return lax.ppermute(block, ("phase", "tile"), route)


def body(volume, frac, shift, angle_index, depth_weights, measured):
    depth, cols, height = volume.shape
    angles = angle_index.shape[1]
    slabs, tiles, phases = (lax.axis_size(a) for a in ("slab", "tile", "phase"))
    group = phases * slabs
    tile = lax.axis_index("tile")
    place = jnp.stack(
        [lax.axis_index("slab"), lax.axis_index("phase"), tile, tile % 2]
    ).astype(jnp.int32)
    octet = pltpu.VMEM((depth, 8, height), F32)
    blocks = pltpu.VMEM((cols // 8, depth, 8, height), F32)
    dma = pltpu.SemaphoreType.DMA

    def toward(phase, tile):
        return phase, tile + 1 - 2 * phase

    def across(phase, tile):
        return 1 - phase, tile - 1 + 2 * phase

    def partner(phase, tile):
        return 1 - phase, tile

    def around(block, distance):
        return lax.ppermute(block, "slab", [(i, (i + distance) % slabs) for i in range(slabs)])

    rim = depth * height // (HALO * LANES)
    bundles = [(angles + 2 + more, size, LANES) for more, size in ((0, cols), (rim, HALO), (0, HALO))]
    message = (slabs, depth, HALO, LANES)
    bundle_own, same, cross, *parts = call(
        load,
        bundles + [message[1:]] * slabs,
        [SMEM] * 2 + [ANY] * 3,
        [octet, dma((slabs + 3,))],
        limit=50,
    )(place, shift, measured, frac, volume)
    index_other = move(angle_index, partner)
    bundle_own, same, cross, index_other, *parts = lax.optimization_barrier(
        (bundle_own, same, cross, index_other, *parts)
    )
    bundle_other = move(bundle_own, partner)
    parts = [parts[0]] + [around(parts[k], k) for k in range(1, slabs)]
    same = move(same, toward)
    cross = move(cross, across)
    wide = pltpu.VMEM((depth, height), F32)
    extras = call(
        pack,
        [(4, depth, LANES)] * slabs,
        [SMEM] + [VMEM] * 4 + [ANY],
        [octet, wide, wide, dma((1,))],
    )(place, angle_index, index_other, same, depth_weights.T, volume)
    extras = [extras[0]] + [around(extras[k], k) for k in range(1, slabs)]
    seen, share, steps = call(
        arrange,
        [(phases, SPAN, angles, LANES), (phases, SPAN, LANES), (phases, SPAN, LANES)],
        [SMEM] + [VMEM] * 4,
    )(place, bundle_own, bundle_other, same, cross)
    steps = steps[:, :, 0].astype(jnp.int32)
    window, side, canvas = (SPAN, LANES), (ROWS, LANES), (4 * HALO, LANES)
    stack = (HALO + 4, 2 * angles, LANES)
    grad, weights, own, other = call(
        core,
        [stack, (2 * angles, LANES), canvas, canvas],
        [SMEM] * 2 + [VMEM] * 10,
        [
            pltpu.VMEM(stack, F32),
            pltpu.VMEM((phases, SPAN, LANES), F32),
            pltpu.VMEM((phases,) + canvas, F32),
            pltpu.VMEM((2, slabs * depth, LANES), F32),
            pltpu.VMEM(message, F32),
        ],
    )(place, steps, *parts, *extras, seen, share)
    (parts,) = call(
        spread,
        [(group, HALO, depth, LANES)],
        [VMEM] * 2,
        [pltpu.VMEM((slabs, HALO, depth, LANES), F32), dma((HALO // 2,))],
        [ANY],
        limit=50,
    )(grad, weights)
    other = move(other, partner)
    parts, other = lax.optimization_barrier((parts, other))
    parts = lax.all_to_all(parts, ("phase", "slab"), 0, 0, tiled=True)
    kept, side_o, side_e = call(merge, [window, side, side], [SMEM] + [VMEM] * 2)(
        place, own, other
    )
    pairs_e = [(i, i ^ 1) for i in range(tiles)]
    pairs_o = [(i, ((i + 1) ^ 1) - 1) for i in range(1, tiles - 1)]
    (field,) = call(collect, [window], [SMEM] + [VMEM] * 3)(
        place, kept, lax.ppermute(side_o, "tile", pairs_o), lax.ppermute(side_e, "tile", pairs_e)
    )
    fields = [field] + [around(field, k) for k in range(1, slabs)]

    def ending(*refs):
        diffuse(tiles - 1, *refs)

    (image,) = call(
        finish, [(depth, cols, height)], [VMEM], [blocks, dma((cols // 8,))], [ANY]
    )(parts)
    image, *fields = lax.optimization_barrier((image, *fields))
    (field,) = call(
        ending,
        [(1, cols, height)],
        [SMEM] + [VMEM] * 4,
        [pltpu.VMEM((slabs,) + window, F32)],
    )(place, *fields)
    return image, field


def solution(mesh):
    return jax.shard_map(
        body,
        mesh=mesh,
        in_specs=(
            P("slab", "tile", None),
            P("phase", "tile", None),
            P("phase", "tile"),
            P("phase", None),
            P(None, "slab"),
            P("phase", None, "tile", None),
        ),
        out_specs=(P("slab", "tile", None), P("phase", "tile", None)),
        check_vma=False,
    )
```
